32 devices in a mesh: fsdp: 16 (over z, x, core), seq: 2 (over y).
Axes of the slice: x: 2, y: 2, z: 4, core: 2. Of those that a mesh axis runs over, the one named last changes fastest.
Arguments:
- tokens: bfloat16 [16, 1024, 1024], P('fsdp', 'seq'), may hold values from -6 to 6
- gain_a: bfloat16 [1024], P(('fsdp', 'seq')), may hold values from 0.5 to 1.5
- mix_in: bfloat16 [1024, 3072], P(('fsdp', 'seq')), may hold values from -0.1875 to 0.1875
- conv_tap: bfloat16 [3, 1024], P(None, ('fsdp', 'seq')), may hold values from -3.5 to 3.5
- mix_out: bfloat16 [1024, 1024], P(('fsdp', 'seq')), may hold values from -0.1875 to 0.1875
- gain_b: bfloat16 [1024], P(('fsdp', 'seq')), may hold values from 0.5 to 1.5
- ff_gate: bfloat16 [1024, 4608], P(('fsdp', 'seq')), may hold values from -0.1875 to 0.1875
- ff_up: bfloat16 [1024, 4608], P(('fsdp', 'seq')), may hold values from -0.1875 to 0.1875
- ff_down: bfloat16 [4608, 1024], P(('fsdp', 'seq')), may hold values from -0.125 to 0.125
- cotangent: bfloat16 [16, 1024, 1024], P('fsdp', 'seq'), may hold values from -6 to 6
Outputs:
- block_out: bfloat16 [16, 1024, 1024], P('fsdp', 'seq')
- grad_tokens: float32 [16, 1024, 1024], P('fsdp', 'seq')
- grad_gain_a: float32 [1024], P(('fsdp', 'seq'))
- grad_mix_in: float32 [1024, 3072], P(('fsdp', 'seq'))
- grad_conv_tap: float32 [3, 1024], P(None, ('fsdp', 'seq'))
- grad_mix_out: float32 [1024, 1024], P(('fsdp', 'seq'))
- grad_gain_b: float32 [1024], P(('fsdp', 'seq'))
- grad_ff_gate: float32 [1024, 4608], P(('fsdp', 'seq'))
- grad_ff_up: float32 [1024, 4608], P(('fsdp', 'seq'))
- grad_ff_down: float32 [4608, 1024], P(('fsdp', 'seq'))
The draws below stay inside these ranges and needn't reach their ends.
All inputs are finite; a program needn't handle non-finite values.
Results may differ from the reference program's by a relative error of at most 0.0096.
Values may be sent and summed in bfloat16 or wider, within the bound.
No kernel may reach another device: no remote copies, remote signals or barrier semaphores. Data moves between devices by JAX's collectives and lax.ppermute only.
A program may use at most 256 MiB of HBM per device.

```python
import math
import jax
import jax.numpy as jnp
from jax import lax

D = 1024
FF = 4608
KW = 3
LEN = 1024
NSEQ = 16


def block_levels(own_key, dims, pieces, smallest, largest):
    factor_of = 1.0
    for position, blocks in pieces:
        steps = jax.random.uniform(jax.random.fold_in(jax.random.fold_in(own_key, 6), position), (blocks,), jnp.float32, smallest / len(pieces), largest / len(pieces))
        factor_of = factor_of * jnp.repeat(jnp.exp(steps), dims[position] // blocks).reshape((-1,) + (1,) * (len(dims) - 1 - position))
    return factor_of


def centred(own_key, shape, scale, reach, pieces=(), held_as=jnp.bfloat16):
    level = block_levels(own_key, shape, pieces, -0.22, 0.18) if pieces else 1.0
    values = jax.random.normal(own_key, shape, jnp.float32) * scale * level
    return jnp.minimum(jnp.maximum(values, -reach), reach).astype(held_as)


def setup_inputs(seed: int = 0) -> dict:
    key_list = jax.random.split(jax.random.key(seed), 11)
    return {
        "tokens": centred(key_list[0], (NSEQ, LEN, D), 1.0, 6.0, ((0, 16), (1, 2))),
        "gain_a": jnp.clip(1.0 + 0.1 * jax.random.normal(key_list[1], (D,), jnp.float32), 0.5, 1.5).astype(jnp.bfloat16),
        "mix_in": centred(key_list[2], (D, 3 * D), D ** -0.5, 0.1875, ((0, 32),)),
        "conv_tap": centred(key_list[3], (KW, D), KW ** -0.5, 3.5, ((1, 32),)),
        "mix_out": centred(key_list[4], (D, D), D ** -0.5, 0.1875, ((0, 32),)),
        "gain_b": jnp.clip(1.0 + 0.1 * jax.random.normal(key_list[5], (D,), jnp.float32), 0.5, 1.5).astype(jnp.bfloat16),
        "ff_gate": centred(key_list[6], (D, FF), D ** -0.5, 0.1875, ((0, 32),)),
        "ff_up": centred(key_list[7], (D, FF), D ** -0.5, 0.1875, ((0, 32),)),
        "ff_down": centred(key_list[8], (FF, D), (FF // 2) ** -0.5, 0.125, ((0, 32),)),
        "cotangent": centred(key_list[9], (NSEQ, LEN, D), 1.0, 6.0, ((0, 16), (1, 2))),
    }


EPSILON = 1e-05

@jax.custom_vjp
def low(v):
    return lax.optimization_barrier(v.astype(jnp.bfloat16)).astype(jnp.float32)

@jax.custom_vjp
def low_back(v):
    return v

def low_keep(v):
    return (low(v), None)

def low_pass(kept, grad):
    return (grad,)

def back_keep(v):
    return (v, None)

def back_low(kept, grad):
    return (low(grad),)
low.defvjp(low_keep, low_pass)
low_back.defvjp(back_keep, back_low)

def norm_rows(values, gain):
    scale = lax.rsqrt(lax.optimization_barrier(jnp.mean(values * values, axis=-1, keepdims=True)) + EPSILON)
    return values * scale * gain

def product(left_segment, right_segment):
    return jnp.einsum('wfc,ci->wfi', left_segment, right_segment, precision=lax.Precision.HIGHEST)

def block_forward_pass(inputs, gain_a, mix_in, conv_tap, mix_out, gain_b, ff_gate, ff_up, ff_down):
    feature_width = inputs.shape[-1]
    length = inputs.shape[1]
    hidden = low(norm_rows(inputs, gain_a))
    projected = low_back(product(hidden, mix_in))
    b_part = projected[..., :feature_width]
    c_part = projected[..., feature_width:2 * feature_width]
    v_part = projected[..., 2 * feature_width:]
    mixed = low(b_part * v_part)
    padded = jnp.pad(mixed, ((0, 0), (KW - 1, 0), (0, 0)))
    convolved = conv_tap[0] * padded[:, 0:length]
    for offset in range(1, KW):
        convolved = convolved + conv_tap[offset] * padded[:, offset:offset + length]
    gated = low(c_part * convolved)
    after_mix = inputs + low_back(product(gated, mix_out))
    hidden_b = low(norm_rows(after_mix, gain_b))
    gate_value = low_back(product(hidden_b, ff_gate))
    up_value = low_back(product(hidden_b, ff_up))
    active = low(jax.nn.silu(gate_value) * up_value)
    return after_mix + low_back(product(active, ff_down))

def reference(tokens, gain_a, mix_in, conv_tap, mix_out, gain_b, ff_gate, ff_up, ff_down, cotangent):
    weights = tuple((weight.astype(jnp.float32) for weight in (gain_a, mix_in, conv_tap, mix_out, gain_b, ff_gate, ff_up, ff_down)))
    per_group = math.gcd(NSEQ, max(1, 4096 // LEN))
    token_groups = tokens.reshape(NSEQ // per_group, per_group, LEN, D)
    cot_groups = cotangent.reshape(NSEQ // per_group, per_group, LEN, D)

    def accumulate(totals, inputs_pair):
        inputs, cot_group = inputs_pair
        results, pullback = jax.vjp(block_forward_pass, inputs.astype(jnp.float32), *weights)
        gradients = pullback(cot_group.astype(jnp.float32))
        totals = tuple((total + gradient for total, gradient in zip(totals, gradients[1:])))
        return (totals, (results.astype(jnp.bfloat16), gradients[0]))
    initial = tuple((jnp.zeros(weight.shape, jnp.float32) for weight in weights))
    totals, (outputs, input_grads) = lax.scan(accumulate, initial, (token_groups, cot_groups))
    return (outputs.reshape(NSEQ, LEN, D), input_grads.reshape(NSEQ, LEN, D), totals[0], totals[1], totals[2], totals[3], totals[4], totals[5], totals[6], totals[7])
```

```python
import jax
import jax.numpy as jnp
from jax import lax
from jax.sharding import PartitionSpec as P

EPSILON = 1e-05
CORE = ("fsdp", 0)


def shifted(shard, axis, by):
    size = lax.axis_size(axis)
    pairs = [(i, i + by) for i in range(size) if 0 <= i + by < size]
    return lax.ppermute(shard, axis, pairs)


def bit_count(axis):
    return lax.axis_size(axis).bit_length() - 1


def my_bit(dim):
    axis, bit = dim
    return (lax.axis_index(axis) >> bit) & 1


def swap(value, dim):
    axis, bit = dim
    return lax.ppermute(value, axis, [(i, i ^ (1 << bit)) for i in range(lax.axis_size(axis))])


def rank(dim):
    axis, bit = dim
    return (0 if axis == "fsdp" else 1, -bit)


def routes():
    near = [("fsdp", b) for b in range(1, min(2, bit_count("fsdp")))]
    far = [("fsdp", b) for b in range(2, bit_count("fsdp"))]
    along = [("seq", b) for b in range(bit_count("seq"))]
    return (far + near + along, far[::-1] + along + near)


def gather_step(buffer, held, dim):
    other = swap(buffer, dim)
    axis = sum(rank(h) < rank(dim) for h in held)
    high = my_bit(dim) == 1
    merged = jnp.stack(
        [jnp.where(high, other, buffer), jnp.where(high, buffer, other)], axis=axis
    )
    return merged, held + [dim]


def gather(piece, held, order):
    held = list(held)
    for dim in order:
        piece, held = gather_step(piece, held, dim)
    return piece


def scatter_step(buffer, held, dim, last):
    axis = sum(rank(h) < rank(dim) for h in held)
    bit = my_bit(dim)
    keep = lax.dynamic_index_in_dim(buffer, bit, axis, keepdims=False)
    send = lax.dynamic_index_in_dim(buffer, 1 - bit, axis, keepdims=False)
    total = keep.astype(jnp.float32) + swap(send, dim).astype(jnp.float32)
    return (total if last else total.astype(jnp.bfloat16)), [h for h in held if h != dim]


def scatter(buffer, held, order):
    held = list(held)
    for step, dim in enumerate(order):
        buffer, held = scatter_step(buffer, held, dim, step == len(order) - 1)
    return buffer


def normalize(values, gain):
    scale = lax.rsqrt(jnp.mean(values * values, axis=-1, keepdims=True) + EPSILON)
    normalized_rows = values * scale
    return (normalized_rows, scale, normalized_rows * gain)


def norm_back(d_hidden, normalized_rows, scale, gain):
    norm_gradient = d_hidden * gain
    grad_gain = jnp.sum(d_hidden * normalized_rows, axis=0)
    d_input = scale * (
        norm_gradient
        - normalized_rows * jnp.mean(norm_gradient * normalized_rows, axis=-1, keepdims=True)
    )
    return (d_input, grad_gain)


def dot_plain(left_segment, right_segment):
    return jnp.dot(left_segment, right_segment, preferred_element_type=jnp.float32)


def dot_first(left_segment, right_segment):
    return lax.dot_general(
        left_segment, right_segment, (((0,), (0,)), ((), ())), preferred_element_type=jnp.float32
    )


def dot_second(left_segment, right_segment):
    return lax.dot_general(
        left_segment, right_segment, (((1,), (1,)), ((), ())), preferred_element_type=jnp.float32
    )


def core_columns(shard, core):
    rows, width = shard.shape
    high = lax.axis_size("fsdp") // 2
    return lax.dynamic_index_in_dim(
        shard.reshape(rows, high, 2, width // (2 * high)), core, 2, keepdims=False
    ).reshape(rows, width // 2)


def body(tokens, gain_a, mix_in, conv_tap, mix_out, gain_b, ff_gate, ff_up, ff_down, cotangent):
    seq_count, local_rows, feature_width = tokens.shape
    row_total = seq_count * local_rows
    tap_count = conv_tap.shape[0]
    own_rows = mix_in.shape[0]
    core = my_bit(CORE)
    route_a, route_b = routes()
    full = 2 * (1 << len(route_a))

    small = jnp.concatenate([gain_a[None], gain_b[None], conv_tap], axis=0).T
    small = jnp.pad(small, ((0, 0), (0, 128 - small.shape[1])))
    half_width = 2 * feature_width
    mixer_a = gather(mix_in[:, :half_width], [], route_a + [CORE])
    mixer_b = gather(
        jnp.concatenate([mix_in[:, half_width:], mix_out, small], axis=1), [], route_b + [CORE]
    )
    weight_bc = mixer_a.reshape(feature_width, half_width)
    mixer_b = mixer_b.reshape(feature_width, half_width + 128)
    weight_v = mixer_b[:, :feature_width]
    weight_out = mixer_b[:, feature_width:half_width]
    small_whole = mixer_b[:, half_width : half_width + 2 + tap_count].T.astype(jnp.float32)
    gain_one, gain_two, tap_values = small_whole[0], small_whole[1], small_whole[2:]

    def gate_like(shard, order):
        mine = core_columns(shard, core)
        piece, held = mine, []
        other = swap(core_columns(shard, 1 - core), CORE)
        high = core == 1
        piece = jnp.stack([jnp.where(high, other, mine), jnp.where(high, mine, other)], axis=0)
        return gather(piece, [CORE], order).reshape(feature_width, -1)

    weight_gate = gate_like(ff_gate, route_a)
    weight_up = gate_like(ff_up, route_b)
    down_half = feature_width // 2
    weight_down_a = gather(ff_down[:, :down_half], [], route_a).reshape(-1, down_half)
    weight_down_b = gather(ff_down[:, down_half:], [], route_b).reshape(-1, down_half)
    weight_down = jnp.concatenate([weight_down_a, weight_down_b], axis=1)

    cot_low = cotangent.reshape(row_total, feature_width)
    cot_full = cot_low.astype(jnp.float32)
    cot_pair = jnp.concatenate([cot_low, swap(cot_low, CORE)], axis=0)

    inputs = tokens.reshape(row_total, feature_width).astype(jnp.float32)
    normed_a, scale_a, hidden = normalize(inputs, gain_one)
    hidden_low = hidden.astype(jnp.bfloat16)
    bc_part = dot_plain(hidden_low, weight_bc)
    b_part = bc_part[:, :feature_width]
    c_part = bc_part[:, feature_width:]
    v_part = dot_plain(hidden_low, weight_v)
    mixed = (b_part * v_part).astype(jnp.bfloat16).reshape(seq_count, local_rows, feature_width)
    edge_rows = shifted(mixed[:, local_rows - (tap_count - 1) :, :], "seq", 1)
    extended = jnp.concatenate([edge_rows, mixed], axis=1).astype(jnp.float32)
    convolved = tap_values[0] * extended[:, 0:local_rows]
    for offset in range(1, tap_count):
        convolved = convolved + tap_values[offset] * extended[:, offset : offset + local_rows]
    convolved = convolved.reshape(row_total, feature_width)
    gated = (c_part * convolved).astype(jnp.bfloat16)
    after_mix = inputs + dot_plain(gated, weight_out)
    normed_b, scale_b, hidden_b = normalize(after_mix, gain_two)
    hidden_b_low = hidden_b.astype(jnp.bfloat16)
    hidden_pair = jnp.concatenate([hidden_b_low, swap(hidden_b_low, CORE)], axis=0)

    gate_value = dot_plain(hidden_pair, weight_gate)
    up_value = dot_plain(hidden_pair, weight_up)
    sigmoid_gate = jax.nn.sigmoid(gate_value)
    silu_gate = gate_value * sigmoid_gate
    active = (silu_gate * up_value).astype(jnp.bfloat16)

    held = [d for d in route_a]
    held_core = held + [CORE]
    shape = (2,) * len(held)
    grad_down = dot_first(active, cot_pair).astype(jnp.bfloat16)
    grad_down = grad_down.reshape(shape + (-1, feature_width))
    down_owned = jnp.concatenate(
        [
            scatter(grad_down[..., :down_half], held, route_a[::-1]),
            scatter(grad_down[..., down_half:], held, route_b[::-1]),
        ],
        axis=-1,
    )

    d_active = dot_second(cot_pair, weight_down)
    d_up = (d_active * silu_gate).astype(jnp.bfloat16)
    d_gate = (
        d_active * up_value * sigmoid_gate * (1.0 + gate_value * (1.0 - sigmoid_gate))
    ).astype(jnp.bfloat16)

    def owned_gate_like(gradient, order):
        gradient = gradient.astype(jnp.bfloat16).reshape(shape + (2, own_rows, -1))
        owned = scatter(gradient, held_core, order)
        mine = lax.dynamic_index_in_dim(owned, core, 0, keepdims=False)
        other = swap(lax.dynamic_index_in_dim(owned, 1 - core, 0, keepdims=False), CORE)
        high = lax.axis_size("fsdp") // 2
        mine, other = (v.reshape(own_rows, high, -1) for v in (mine, other))
        both = jnp.stack(
            [jnp.where(core == 1, other, mine), jnp.where(core == 1, mine, other)], axis=2
        )
        return both.reshape(own_rows, -1)

    up_owned = owned_gate_like(dot_first(hidden_pair, d_up), route_b[::-1])
    gate_owned = owned_gate_like(dot_first(hidden_pair, d_gate), route_a[::-1])

    d_hidden_pair = dot_second(d_gate, weight_gate) + dot_second(d_up, weight_up)
    d_hidden_b = d_hidden_pair[:row_total] + swap(d_hidden_pair[row_total:], CORE)
    d_norm_input, grad_gain_two = norm_back(d_hidden_b, normed_b, scale_b, gain_two)
    d_after = cot_full + d_norm_input

    out_pair = dot_plain(active, weight_down)
    results = after_mix + out_pair[:row_total] + swap(out_pair[row_total:], CORE)
    block_out = results.astype(jnp.bfloat16).reshape(seq_count, local_rows, feature_width)

    d_branch = d_after.astype(jnp.bfloat16)
    d_gated = dot_second(d_branch, weight_out)
    d_c_part = d_gated * convolved
    d_conv = (d_gated * c_part).reshape(seq_count, local_rows, feature_width)
    grad_taps = jnp.stack(
        [
            jnp.sum(d_conv * extended[:, offset : offset + local_rows], axis=(0, 1))
            for offset in range(tap_count)
        ],
        axis=0,
    )
    padded_grad = jnp.pad(d_conv, ((0, 0), (tap_count - 1, tap_count - 1), (0, 0)))
    span = local_rows + tap_count - 1
    d_extended = tap_values[0] * padded_grad[:, tap_count - 1 : tap_count - 1 + span]
    for offset in range(1, tap_count):
        start_at = tap_count - 1 - offset
        d_extended = d_extended + tap_values[offset] * padded_grad[:, start_at : start_at + span]
    incoming = shifted(d_extended[:, : tap_count - 1, :], "seq", -1)
    incoming_full = jnp.pad(incoming, ((0, 0), (local_rows - (tap_count - 1), 0), (0, 0)))
    d_mixed = (d_extended[:, tap_count - 1 :, :] + incoming_full).reshape(row_total, feature_width)
    d_b = (d_mixed * v_part).astype(jnp.bfloat16)
    d_c = d_c_part.astype(jnp.bfloat16)
    d_v = (d_mixed * b_part).astype(jnp.bfloat16)
    d_bc = jnp.concatenate([d_b, d_c], axis=1)
    grad_a = dot_first(hidden_low, d_bc).astype(jnp.bfloat16)
    grad_b = jnp.concatenate(
        [
            dot_first(gated, d_branch).astype(jnp.bfloat16),
            dot_first(hidden_low, d_v).astype(jnp.bfloat16),
        ],
        axis=1,
    )
    shape_all = (2,) * len(held_core) + (own_rows, half_width)
    owned_a = scatter(grad_a.reshape(shape_all), held_core, [CORE] + route_a[::-1])
    owned_b = scatter(grad_b.reshape(shape_all), held_core, [CORE] + route_b[::-1])

    d_hidden = dot_second(d_bc, weight_bc) + dot_second(d_v, weight_v)
    d_first_norm, grad_gain_one = norm_back(d_hidden, normed_a, scale_a, gain_one)
    grad_tokens = (d_after + d_first_norm).reshape(seq_count, local_rows, feature_width)
    small_terms = jnp.concatenate(
        [grad_gain_one[None, :], grad_gain_two[None, :], grad_taps], axis=0
    )
    for dim in [CORE] + route_a:
        small_terms = small_terms + swap(small_terms, dim)
    place = lax.axis_index("fsdp") * lax.axis_size("seq") + lax.axis_index("seq")
    small_owned = lax.dynamic_slice_in_dim(small_terms, place * own_rows, own_rows, axis=1)
    return (
        block_out,
        grad_tokens,
        small_owned[0],
        jnp.concatenate([owned_a, owned_b[:, feature_width:]], axis=1),
        small_owned[2:],
        owned_b[:, :feature_width],
        small_owned[1],
        gate_owned,
        up_owned,
        down_owned,
    )


def solution(mesh):
    return jax.shard_map(
        body,
        mesh=mesh,
        in_specs=(
            P("fsdp", "seq", None),
            P(("fsdp", "seq")),
            P(("fsdp", "seq"), None),
            P(None, ("fsdp", "seq")),
            P(("fsdp", "seq"), None),
            P(("fsdp", "seq")),
            P(("fsdp", "seq"), None),
            P(("fsdp", "seq"), None),
            P(("fsdp", "seq"), None),
            P("fsdp", "seq", None),
        ),
        out_specs=(
            P("fsdp", "seq", None),
            P("fsdp", "seq", None),
            P(("fsdp", "seq")),
            P(("fsdp", "seq"), None),
            P(None, ("fsdp", "seq")),
            P(("fsdp", "seq"), None),
            P(("fsdp", "seq")),
            P(("fsdp", "seq"), None),
            P(("fsdp", "seq"), None),
            P(("fsdp", "seq"), None),
        ),
        check_vma=False,
    )
```

```python
import jax
import jax.numpy as jnp
from jax import lax
from jax.sharding import PartitionSpec as P

EPSILON = 1e-05
CORE = ("fsdp", 0)
SIDE = ("seq", 0)


def shifted(shard, axis, by):
    size = lax.axis_size(axis)
    pairs = [(i, i + by) for i in range(size) if 0 <= i + by < size]
    return lax.ppermute(shard, axis, pairs)


def bit_count(axis):
    return lax.axis_size(axis).bit_length() - 1


def my_bit(dim):
    axis, bit = dim
    return (lax.axis_index(axis) >> bit) & 1


def swap(value, dim):
    axis, bit = dim
    return lax.ppermute(value, axis, [(i, i ^ (1 << bit)) for i in range(lax.axis_size(axis))])


def rank(dim):
    axis, bit = dim
    return (0 if axis == "fsdp" else 1, -bit)


def down_rank(dim):
    top = bit_count("fsdp") - 1
    return rank({("fsdp", top): CORE, ("fsdp", top - 1): SIDE}.get(dim, dim))


def tie(*values):
    return lax.optimization_barrier(values)


class Gather:
    def __init__(self, piece, dims, held=(), order=rank):
        self.buffer, self.left, self.held, self.order = piece, list(dims), list(held), order

    def step(self):
        if not self.left:
            return
        dim = self.left.pop(0)
        other, mine = swap(self.buffer, dim), self.buffer
        axis = sum(self.order(h) < self.order(dim) for h in self.held)
        high = my_bit(dim) == 1
        self.buffer = jnp.stack(
            [jnp.where(high, other, mine), jnp.where(high, mine, other)], axis=axis
        )
        self.held.append(dim)


class Scatter:
    def __init__(self, terms, dims, held, order=rank):
        self.buffer, self.left, self.order = terms, list(dims), order
        self.held = sorted(held, key=order)

    def step(self):
        if not self.left:
            return
        dim = self.left.pop(0)
        axis = self.held.index(dim)
        bit = my_bit(dim)
        keep = lax.dynamic_index_in_dim(self.buffer, bit, axis, keepdims=False)
        send = lax.dynamic_index_in_dim(self.buffer, 1 - bit, axis, keepdims=False)
        total = keep.astype(jnp.float32) + swap(send, dim).astype(jnp.float32)
        self.buffer = total.astype(jnp.bfloat16) if self.left else total
        self.held.remove(dim)


def advance(chains, *others):
    for chain in chains:
        chain.step()
    tied = tie(*(chain.buffer for chain in chains), *others)
    for chain, buffer in zip(chains, tied):
        chain.buffer = buffer
    return tied[len(chains) :]


def finish(*chains):
    for chain in chains:
        while chain.left:
            chain.step()


def normalize(values, gain):
    scale = lax.rsqrt(jnp.mean(values * values, axis=-1, keepdims=True) + EPSILON)
    normalized_rows = values * scale
    return (normalized_rows, scale, normalized_rows * gain)


def norm_back(d_hidden, normalized_rows, scale, gain):
    norm_gradient = d_hidden * gain
    grad_gain = jnp.sum(d_hidden * normalized_rows, axis=0)
    d_input = scale * (
        norm_gradient
        - normalized_rows * jnp.mean(norm_gradient * normalized_rows, axis=-1, keepdims=True)
    )
    return (d_input, grad_gain)


def dot_plain(left_segment, right_segment):
    return jnp.dot(left_segment, right_segment, preferred_element_type=jnp.float32)


def dot_first(left_segment, right_segment):
    return lax.dot_general(
        left_segment, right_segment, (((0,), (0,)), ((), ())), preferred_element_type=jnp.float32
    )


def dot_second(left_segment, right_segment):
    return lax.dot_general(
        left_segment, right_segment, (((1,), (1,)), ((), ())), preferred_element_type=jnp.float32
    )


def quarter_owner_swap(value):
    fsdp, seq = lax.axis_size("fsdp"), lax.axis_size("seq")
    top = bit_count("fsdp") - 1
    pairs = []
    for device in range(fsdp * seq):
        f, s = divmod(device, seq)
        high, low = (f >> top) & 1, (f >> (top - 1)) & 1
        core, side = f & 1, s & 1
        f2 = (f & ~((1 << top) | (1 << (top - 1)) | 1)) | (core << top) | (side << (top - 1)) | high
        pairs.append((device, f2 * seq + ((s & ~1) | low)))
    return lax.ppermute(value, ("fsdp", "seq"), pairs)


def body(tokens, gain_a, mix_in, conv_tap, mix_out, gain_b, ff_gate, ff_up, ff_down, cotangent):
    seq_count, local_rows, feature_width = tokens.shape
    row_total = seq_count * local_rows
    pair_rows = 2 * row_total
    tap_count = conv_tap.shape[0]
    own_rows = mix_in.shape[0]
    hidden_units = ff_gate.shape[1]
    quarter = hidden_units // 4
    core, side = my_bit(CORE), my_bit(SIDE)
    near = [("fsdp", 1)]
    far = [("fsdp", b) for b in range(2, bit_count("fsdp"))]
    outer = [("seq", b) for b in range(1, bit_count("seq"))]
    zx, zx_turned = far + near + outer, far[::-1] + near + outer
    route_a, route_b = far + near + outer + [SIDE], far[::-1] + [SIDE] + outer + near
    group = [CORE, SIDE]
    half_width = 2 * feature_width
    down_half = feature_width // 2

    def ordered(pair_bit, mine, other):
        high = pair_bit == 1
        return jnp.where(high, other, mine), jnp.where(high, mine, other)

    small = jnp.concatenate([gain_a[None], gain_b[None], conv_tap], axis=0).T
    small = jnp.pad(small, ((0, 0), (0, 128 - small.shape[1])))
    mix_a = Gather(
        jnp.concatenate([mix_in[:, :feature_width], mix_in[:, 2 * feature_width :]], axis=1), route_a
    )
    mix_b = Gather(
        jnp.concatenate([mix_in[:, feature_width : 2 * feature_width], mix_out, small], axis=1),
        route_b,
    )
    down_x = Gather(ff_down, near + outer)

    def quarters(shard):
        return jnp.stack([shard[:, q * quarter : (q + 1) * quarter] for q in range(4)]).reshape(
            2, 2, own_rows, quarter
        )

    def regroup(parts, axis, bit, dim):
        mine = lax.dynamic_index_in_dim(parts, bit, axis, keepdims=False)
        other = swap(lax.dynamic_index_in_dim(parts, 1 - bit, axis, keepdims=False), dim)
        return mine, other

    gate_mine, gate_other = regroup(quarters(ff_gate), 1, side, SIDE)
    up_mine, up_other = regroup(quarters(ff_up), 1, side, SIDE)
    cot_low = cotangent.reshape(row_total, feature_width)
    cot_first, cot_last = cot_low[: row_total // 2], cot_low[row_total // 2 :]
    gate_mine, gate_other, up_mine, up_other, cot_first = advance(
        [mix_a, mix_b, down_x], gate_mine, gate_other, up_mine, up_other, cot_first
    )

    def regroup_core(mine, other):
        both = jnp.stack(ordered(side, mine, other), axis=1)
        return jnp.stack(ordered(core, *regroup(both, 0, core, CORE)), axis=0)

    gate = Gather(regroup_core(gate_mine, gate_other), zx, group)
    up = Gather(regroup_core(up_mine, up_other), zx_turned, group)
    cot_first_other = swap(cot_first, SIDE)
    gate.buffer, up.buffer, cot_first_other, cot_last = advance(
        [mix_a, mix_b], gate.buffer, up.buffer, cot_first_other, cot_last
    )

    while mix_a.left or mix_b.left:
        advance([mix_a, mix_b, gate, up])

    inputs = tokens.reshape(row_total, feature_width).astype(jnp.float32)
    cot_full = cot_low.astype(jnp.float32)
    core_a, core_b = Gather(mix_a.buffer, [CORE], mix_a.held), Gather(mix_b.buffer, [CORE], mix_b.held)
    core_a.step()
    core_b.step()
    weight_bv = core_a.buffer.reshape(feature_width, half_width)
    weight_c_out = core_b.buffer.reshape(feature_width, half_width + 128)
    weight_c = weight_c_out[:, :feature_width]
    weight_out = weight_c_out[:, feature_width:half_width]
    small_whole = weight_c_out[:, half_width : half_width + 2 + tap_count].T.astype(jnp.float32)
    gain_one, gain_two, tap_values = small_whole[0], small_whole[1], small_whole[2:]
    normed_a, scale_a, hidden = normalize(inputs, gain_one)
    hidden_low = hidden.astype(jnp.bfloat16)
    bv_part = dot_plain(hidden_low, weight_bv)
    b_part = bv_part[:, :feature_width]
    v_part = bv_part[:, feature_width:]
    mixed = (b_part * v_part).astype(jnp.bfloat16).reshape(seq_count, local_rows, feature_width)
    edge_rows = shifted(mixed[:, local_rows - (tap_count - 1) :, :], "seq", 1)
    c_part = dot_plain(hidden_low, weight_c)
    edge_rows, cot_last = tie(edge_rows, cot_last)
    cot_last_other = swap(cot_last, SIDE)
    extended = jnp.concatenate([edge_rows, mixed], axis=1).astype(jnp.float32)
    convolved = tap_values[0] * extended[:, 0:local_rows]
    for offset in range(1, tap_count):
        convolved = convolved + tap_values[offset] * extended[:, offset : offset + local_rows]
    convolved = convolved.reshape(row_total, feature_width)
    gated = (c_part * convolved).astype(jnp.bfloat16)
    after_mix = inputs + dot_plain(gated, weight_out)
    normed_b, scale_b, hidden_b = normalize(after_mix, gain_two)
    hidden_b_low = hidden_b.astype(jnp.bfloat16)
    finish(down_x)
    down_piece = quarter_owner_swap(down_x.buffer)
    down_a = Gather(down_piece[..., :down_half], far, near + outer, down_rank)
    down_b = Gather(down_piece[..., down_half:], far[::-1], near + outer, down_rank)
    hidden_b_low, cot_last_other = advance(
        [gate, down_a, down_b], hidden_b_low, cot_last_other
    )
    finish(gate)

    hidden_two = jnp.concatenate([hidden_b_low, swap(hidden_b_low, SIDE)], axis=0)
    hidden_four = jnp.concatenate([hidden_two, swap(hidden_two, CORE)], axis=0)
    cot_two = jnp.concatenate([cot_low, cot_first_other, cot_last_other], axis=0)
    cot_four = jnp.concatenate([cot_two, swap(cot_two, CORE)], axis=0)
    hidden_four, cot_four = advance([up, down_a, down_b], hidden_four, cot_four)
    finish(up, down_a, down_b)
    weight_gate = gate.buffer.reshape(feature_width, quarter)
    weight_up = up.buffer.reshape(feature_width, quarter)
    weight_down = jnp.concatenate(
        [down_a.buffer.reshape(quarter, down_half), down_b.buffer.reshape(quarter, down_half)], axis=1
    )

    gate_value = dot_plain(hidden_four, weight_gate)
    up_value = dot_plain(hidden_four, weight_up)
    sigmoid_gate = jax.nn.sigmoid(gate_value)
    silu_gate = gate_value * sigmoid_gate
    active = (silu_gate * up_value).astype(jnp.bfloat16)

    def split(gradient, rows):
        return gradient.astype(jnp.bfloat16).reshape((2,) * len(zx) + rows)

    grad_down = split(dot_first(active, cot_four), (-1, feature_width))
    grad_down, cot_four = tie(grad_down, cot_four)
    grad_down_a = Scatter(grad_down[..., :down_half], zx[::-1], zx, down_rank)
    grad_down_b = Scatter(grad_down[..., down_half:], zx_turned[::-1], zx, down_rank)

    d_active = dot_second(cot_four, weight_down)
    d_up = (d_active * silu_gate).astype(jnp.bfloat16)
    d_gate = (
        d_active * up_value * sigmoid_gate * (1.0 + gate_value * (1.0 - sigmoid_gate))
    ).astype(jnp.bfloat16)

    def two_rows(parts):
        def rows(at):
            return sum(dot(left[at], right) for dot, left, right in parts)

        far_rows = rows(slice(pair_rows, None)).astype(jnp.bfloat16)
        two = rows(slice(0, pair_rows)) + swap(far_rows, CORE).astype(jnp.float32)
        return two[:row_total], two[row_total:].astype(jnp.bfloat16)

    d_hidden_own, d_hidden_far = two_rows(
        [(dot_second, d_gate, weight_gate), (dot_second, d_up, weight_up)]
    )
    d_hidden_own, d_hidden_far, d_gate, d_up = tie(d_hidden_own, d_hidden_far, d_gate, d_up)
    gate_rows = (2, 2, own_rows, quarter)
    grad_gate = Scatter(split(dot_first(hidden_four, d_gate), gate_rows), zx[::-1], zx + group)
    grad_gate.buffer, d_hidden_own, d_hidden_far, d_up, active = advance(
        [grad_down_a, grad_down_b], grad_gate.buffer, d_hidden_own, d_hidden_far, d_up, active
    )

    d_hidden_b = d_hidden_own + swap(d_hidden_far, SIDE).astype(jnp.float32)
    grad_up = Scatter(
        split(dot_first(hidden_four, d_up), gate_rows), zx_turned[::-1], zx + group
    )
    out_own, out_far = two_rows([(dot_plain, active, weight_down)])
    d_hidden_b, grad_up.buffer, out_own, out_far = advance(
        [grad_gate, grad_down_a, grad_down_b], d_hidden_b, grad_up.buffer, out_own, out_far
    )

    d_norm_input, grad_gain_two = norm_back(d_hidden_b, normed_b, scale_b, gain_two)
    d_after = cot_full + d_norm_input
    d_branch = d_after.astype(jnp.bfloat16)
    d_gated = dot_second(d_branch, weight_out)
    d_c = (d_gated * convolved).astype(jnp.bfloat16)
    d_conv = (d_gated * c_part).reshape(seq_count, local_rows, feature_width)
    padded_grad = jnp.pad(d_conv, ((0, 0), (tap_count - 1, tap_count - 1), (0, 0)))
    span = local_rows + tap_count - 1
    d_extended = tap_values[0] * padded_grad[:, tap_count - 1 : tap_count - 1 + span]
    for offset in range(1, tap_count):
        start_at = tap_count - 1 - offset
        d_extended = d_extended + tap_values[offset] * padded_grad[:, start_at : start_at + span]
    incoming = shifted(d_extended[:, : tap_count - 1, :], "seq", -1)
    incoming, out_far = tie(incoming, out_far)
    out_other = swap(out_far, SIDE).astype(jnp.float32)
    results = after_mix + (out_own + out_other)
    block_out = results.astype(jnp.bfloat16).reshape(seq_count, local_rows, feature_width)
    held_all = route_a + [CORE]
    shape_all = (2,) * len(held_all) + (own_rows, half_width)
    terms_b = jnp.concatenate(
        [
            dot_first(gated, d_branch).astype(jnp.bfloat16),
            dot_first(hidden_low, d_c).astype(jnp.bfloat16),
        ],
        axis=1,
    )
    grad_b = Scatter(terms_b.reshape(shape_all), [CORE] + route_b[::-1], held_all)
    grad_b.step()
    incoming_full = jnp.pad(incoming, ((0, 0), (local_rows - (tap_count - 1), 0), (0, 0)))
    d_mixed = (d_extended[:, tap_count - 1 :, :] + incoming_full).reshape(row_total, feature_width)
    d_bv = jnp.concatenate(
        [(d_mixed * v_part).astype(jnp.bfloat16), (d_mixed * b_part).astype(jnp.bfloat16)], axis=1
    )
    grad_a = Scatter(
        dot_first(hidden_low, d_bv).astype(jnp.bfloat16).reshape(shape_all),
        [CORE] + route_a[::-1],
        held_all,
    )
    grad_a.step()
    d_bv, d_c, d_conv, block_out, grad_a.buffer, grad_b.buffer = advance(
        [grad_up, grad_gate, grad_down_a, grad_down_b],
        d_bv, d_c, d_conv, block_out, grad_a.buffer, grad_b.buffer,
    )
    finish(grad_down_a, grad_down_b)
    down_owned = quarter_owner_swap(
        jnp.concatenate([grad_down_a.buffer, grad_down_b.buffer], axis=-1)
    )

    grad_taps = jnp.stack(
        [
            jnp.sum(d_conv * extended[:, offset : offset + local_rows], axis=(0, 1))
            for offset in range(tap_count)
        ],
        axis=0,
    )
    d_hidden = dot_second(d_bv, weight_bv) + dot_second(d_c, weight_c)
    d_first_norm, grad_gain_one = norm_back(d_hidden, normed_a, scale_a, gain_one)
    grad_tokens = (d_after + d_first_norm).reshape(seq_count, local_rows, feature_width)
    small_terms = jnp.concatenate(
        [grad_gain_one[None, :], grad_gain_two[None, :], grad_taps], axis=0
    )
    small_terms, grad_tokens, down_owned = advance(
        [grad_a, grad_b, grad_up, grad_gate], small_terms, grad_tokens, down_owned
    )
    finish(grad_gate)

    def owned_quarters(owned):
        both = jnp.stack(ordered(core, *regroup(owned, 0, core, CORE)), axis=1)
        mine = lax.dynamic_index_in_dim(both, side, 0, keepdims=False)
        send = lax.dynamic_index_in_dim(both, 1 - side, 0, keepdims=False)
        other = swap(send.astype(jnp.bfloat16), SIDE).astype(jnp.float32)
        low, high = ordered(side, mine, other)
        return jnp.concatenate([low[0], high[0], low[1], high[1]], axis=-1)

    gate_owned = owned_quarters(grad_gate.buffer)
    advance([grad_a, grad_b, grad_up])
    finish(grad_up)
    up_owned = owned_quarters(grad_up.buffer)
    for dim in [CORE] + route_a:
        small_terms = small_terms + swap(small_terms, dim)
    while grad_a.left or grad_b.left:
        advance([grad_a, grad_b])
    owned_a, owned_b = grad_a.buffer, grad_b.buffer
    place = lax.axis_index("fsdp") * lax.axis_size("seq") + lax.axis_index("seq")
    small_owned = lax.dynamic_slice_in_dim(small_terms, place * own_rows, own_rows, axis=1)
    return (
        block_out,
        grad_tokens,
        small_owned[0],
        jnp.concatenate(
            [owned_a[:, :feature_width], owned_b[:, feature_width:], owned_a[:, feature_width:]],
            axis=1,
        ),
        small_owned[2:],
        owned_b[:, :feature_width],
        small_owned[1],
        gate_owned,
        up_owned,
        down_owned,
    )


def solution(mesh):
    return jax.shard_map(
        body,
        mesh=mesh,
        in_specs=(
            P("fsdp", "seq", None),
            P(("fsdp", "seq")),
            P(("fsdp", "seq"), None),
            P(None, ("fsdp", "seq")),
            P(("fsdp", "seq"), None),
            P(("fsdp", "seq")),
            P(("fsdp", "seq"), None),
            P(("fsdp", "seq"), None),
            P(("fsdp", "seq"), None),
            P("fsdp", "seq", None),
        ),
        out_specs=(
            P("fsdp", "seq", None),
            P("fsdp", "seq", None),
            P(("fsdp", "seq")),
            P(("fsdp", "seq"), None),
            P(None, ("fsdp", "seq")),
            P(("fsdp", "seq"), None),
            P(("fsdp", "seq")),
            P(("fsdp", "seq"), None),
            P(("fsdp", "seq"), None),
            P(("fsdp", "seq"), None),
        ),
        check_vma=False,
    )
```

```python
import jax
import jax.numpy as jnp
from jax import lax
from jax.sharding import PartitionSpec as P

EPSILON = 1e-05
CORE = ("fsdp", 0)
SIDE = ("seq", 0)


def shifted(shard, axis, by):
    size = lax.axis_size(axis)
    pairs = [(i, i + by) for i in range(size) if 0 <= i + by < size]
    return lax.ppermute(shard, axis, pairs)


def bit_count(axis):
    return lax.axis_size(axis).bit_length() - 1


def my_bit(dim):
    axis, bit = dim
    return (lax.axis_index(axis) >> bit) & 1


def swap(value, dim):
    axis, bit = dim
    return lax.ppermute(value, axis, [(i, i ^ (1 << bit)) for i in range(lax.axis_size(axis))])


def rank(dim):
    axis, bit = dim
    return (0 if axis == "fsdp" else 1, -bit)


def down_rank(dim):
    top = bit_count("fsdp") - 1
    return rank({("fsdp", top): CORE, ("fsdp", top - 1): SIDE}.get(dim, dim))


def tie(*values):
    return lax.optimization_barrier(values)


class Chain:
    def __init__(self, buffer, dims, held, order):
        self.buffer, self.left, self.held, self.order = buffer, list(dims), list(held), order
        self.parts = []

    def start(self):
        if self.left:
            self.parts = [swap(self.sent(), self.left[0])]

    def start_half(self, half):
        if self.left:
            sent = self.sent()
            middle = sent.shape[0] // 2
            part = swap(sent[middle:] if half else sent[:middle], self.left[0])
            self.parts = self.parts + [part] if half else [part]

    def merge(self):
        if self.left:
            other = self.parts[0] if len(self.parts) == 1 else jnp.concatenate(self.parts, axis=0)
            self.parts = []
            self.take(self.left.pop(0), other)


class Gather(Chain):
    def __init__(self, piece, dims, held=(), order=rank):
        super().__init__(piece, dims, held, order)

    def sent(self):
        return self.buffer

    def take(self, dim, other):
        axis = sum(self.order(h) < self.order(dim) for h in self.held)
        high = my_bit(dim) == 1
        self.buffer = jnp.stack(
            [jnp.where(high, other, self.buffer), jnp.where(high, self.buffer, other)], axis=axis
        )
        self.held.append(dim)


class Scatter(Chain):
    def __init__(self, terms, dims, held, order=rank):
        super().__init__(terms, dims, sorted(held, key=order), order)

    def sent(self):
        axis, bit = self.held.index(self.left[0]), my_bit(self.left[0])
        return lax.dynamic_index_in_dim(self.buffer, 1 - bit, axis, keepdims=False)

    def take(self, dim, other):
        axis, bit = self.held.index(dim), my_bit(dim)
        keep = lax.dynamic_index_in_dim(self.buffer, bit, axis, keepdims=False)
        total = keep.astype(jnp.float32) + other.astype(jnp.float32)
        self.buffer = total.astype(jnp.bfloat16) if self.left else total
        self.held.remove(dim)


def tie_chains(chains, *others, parts=True):
    count = [len(chain.parts) if parts else 0 for chain in chains]
    flat = [p for chain, n in zip(chains, count) for p in chain.parts[:n]]
    tied = list(tie(*(chain.buffer for chain in chains), *flat, *others))
    for chain in chains:
        chain.buffer = tied.pop(0)
    for chain, n in zip(chains, count):
        chain.parts = [tied.pop(0) for _ in range(n)] + chain.parts[n:]
    return tied


def advance(chains, *others, first=(), second=()):
    for chain in chains:
        chain.start()
    for chain in first:
        chain.start_half(0)
    for chain in second:
        chain.start_half(1)
    every = [*chains, *first, *second]
    others = tie_chains(every, *others, parts=False)
    for chain in [*chains, *second]:
        chain.merge()
    return tie_chains(every, *others)


def step(chain):
    chain.start()
    chain.merge()


def finish(*chains):
    for chain in chains:
        while chain.left:
            step(chain)


def normalize(values, gain):
    scale = lax.rsqrt(jnp.mean(values * values, axis=-1, keepdims=True) + EPSILON)
    normalized_rows = values * scale
    return (normalized_rows, scale, normalized_rows * gain)


def norm_back(d_hidden, normalized_rows, scale, gain):
    norm_gradient = d_hidden * gain
    grad_gain = jnp.sum(d_hidden * normalized_rows, axis=0)
    d_input = scale * (
        norm_gradient
        - normalized_rows * jnp.mean(norm_gradient * normalized_rows, axis=-1, keepdims=True)
    )
    return (d_input, grad_gain)


def dot_plain(left_segment, right_segment):
    return jnp.dot(left_segment, right_segment, preferred_element_type=jnp.float32)


def dot_first(left_segment, right_segment):
    return lax.dot_general(
        left_segment, right_segment, (((0,), (0,)), ((), ())), preferred_element_type=jnp.float32
    )


def dot_second(left_segment, right_segment):
    return lax.dot_general(
        left_segment, right_segment, (((1,), (1,)), ((), ())), preferred_element_type=jnp.float32
    )


def quarter_owner_swap(value):
    fsdp, seq = lax.axis_size("fsdp"), lax.axis_size("seq")
    top = bit_count("fsdp") - 1
    pairs = []
    for device in range(fsdp * seq):
        f, s = divmod(device, seq)
        high, low = (f >> top) & 1, (f >> (top - 1)) & 1
        core, side = f & 1, s & 1
        f2 = (f & ~((1 << top) | (1 << (top - 1)) | 1)) | (core << top) | (side << (top - 1)) | high
        pairs.append((device, f2 * seq + ((s & ~1) | low)))
    return lax.ppermute(value, ("fsdp", "seq"), pairs)


def body(tokens, gain_a, mix_in, conv_tap, mix_out, gain_b, ff_gate, ff_up, ff_down, cotangent):
    seq_count, local_rows, feature_width = tokens.shape
    row_total = seq_count * local_rows
    tap_count = conv_tap.shape[0]
    own_rows = mix_in.shape[0]
    hidden_units = ff_gate.shape[1]
    quarter = hidden_units // 4
    core, side = my_bit(CORE), my_bit(SIDE)
    near = [("fsdp", 1)]
    far = [("fsdp", b) for b in range(2, bit_count("fsdp"))]
    outer = [("seq", b) for b in range(1, bit_count("seq"))]
    zx, zx_turned = far + near + outer, far[::-1] + near + outer
    route_a, route_b = far + near + outer + [SIDE], far[::-1] + [SIDE] + outer + near
    group = [CORE, SIDE]
    half_width = 2 * feature_width
    down_half = feature_width // 2

    def ordered(pair_bit, mine, other):
        high = pair_bit == 1
        return jnp.where(high, other, mine), jnp.where(high, mine, other)

    small = jnp.concatenate([gain_a[None], gain_b[None], conv_tap], axis=0).T
    small = jnp.pad(small, ((0, 0), (0, 128 - small.shape[1])))
    mix_a = Gather(
        jnp.concatenate([mix_in[:, :feature_width], mix_in[:, 2 * feature_width :]], axis=1), route_a
    )
    mix_b = Gather(
        jnp.concatenate([mix_in[:, feature_width : 2 * feature_width], mix_out, small], axis=1),
        route_b,
    )
    down_piece = quarter_owner_swap(ff_down)

    def quarters(shard):
        return jnp.stack([shard[:, q * quarter : (q + 1) * quarter] for q in range(4)]).reshape(
            2, 2, own_rows, quarter
        )

    def regroup(parts, axis, bit, dim):
        mine = lax.dynamic_index_in_dim(parts, bit, axis, keepdims=False)
        other = swap(lax.dynamic_index_in_dim(parts, 1 - bit, axis, keepdims=False), dim)
        return mine, other

    gate_mine, gate_other = regroup(quarters(ff_gate), 1, side, SIDE)
    up_mine, up_other = regroup(quarters(ff_up), 1, side, SIDE)
    cot_low = cotangent.reshape(row_total, feature_width)
    cot_first, cot_last = cot_low[: row_total // 2], cot_low[row_total // 2 :]
    gate_mine, gate_other, up_mine, up_other, cot_first, down_piece = advance(
        [mix_a, mix_b], gate_mine, gate_other, up_mine, up_other, cot_first, down_piece
    )
    down_x = Gather(down_piece, near + outer, (), down_rank)

    def regroup_core(mine, other):
        both = jnp.stack(ordered(side, mine, other), axis=1)
        return jnp.stack(ordered(core, *regroup(both, 0, core, CORE)), axis=0)

    gate = Gather(regroup_core(gate_mine, gate_other), zx_turned, group)
    up = Gather(regroup_core(up_mine, up_other), zx, group)
    cot_first_other = swap(cot_first, SIDE)
    gate.buffer, up.buffer, cot_first_other, cot_last = advance(
        [mix_a, mix_b, down_x], gate.buffer, up.buffer, cot_first_other, cot_last
    )

    finish(down_x)
    while mix_a.left or mix_b.left:
        down_x.buffer, cot_last = advance([mix_a, mix_b, gate, up], down_x.buffer, cot_last)

    inputs = tokens.reshape(row_total, feature_width).astype(jnp.float32)
    cot_full = cot_low.astype(jnp.float32)
    cot_last_other = swap(cot_last, SIDE)
    core_a, core_b = Gather(mix_a.buffer, [CORE], mix_a.held), Gather(mix_b.buffer, [CORE], mix_b.held)
    step(core_a)
    step(core_b)
    weight_bv = core_a.buffer.reshape(feature_width, half_width)
    weight_c_out = core_b.buffer.reshape(feature_width, half_width + 128)
    weight_c = weight_c_out[:, :feature_width]
    weight_out = weight_c_out[:, feature_width:half_width]
    small_whole = weight_c_out[:, half_width : half_width + 2 + tap_count].T.astype(jnp.float32)
    gain_one, gain_two, tap_values = small_whole[0], small_whole[1], small_whole[2:]
    normed_a, scale_a, hidden = normalize(inputs, gain_one)
    hidden_low = hidden.astype(jnp.bfloat16)
    bv_part = dot_plain(hidden_low, weight_bv)
    b_part = bv_part[:, :feature_width]
    v_part = bv_part[:, feature_width:]
    mixed = (b_part * v_part).astype(jnp.bfloat16).reshape(seq_count, local_rows, feature_width)
    mixed, hidden_low, weight_c, down_piece, cot_last_other = advance(
        [], mixed, hidden_low, weight_c, down_x.buffer, cot_last_other, first=[gate]
    )
    edge_rows = shifted(mixed[:, local_rows - (tap_count - 1) :, :], "seq", 1)
    c_part = dot_plain(hidden_low, weight_c)
    extended = jnp.concatenate([edge_rows, mixed], axis=1).astype(jnp.float32)
    convolved = tap_values[0] * extended[:, 0:local_rows]
    for offset in range(1, tap_count):
        convolved = convolved + tap_values[offset] * extended[:, offset : offset + local_rows]
    convolved = convolved.reshape(row_total, feature_width)
    gated = (c_part * convolved).astype(jnp.bfloat16)
    after_mix = inputs + dot_plain(gated, weight_out)
    normed_b, scale_b, hidden_b = normalize(after_mix, gain_two)
    hidden_b_low = hidden_b.astype(jnp.bfloat16)
    down_a = Gather(down_piece[..., :down_half], far, near + outer, down_rank)
    down_b = Gather(down_piece[..., down_half:], far[::-1], near + outer, down_rank)
    (hidden_b_low,) = advance([down_a, down_b], hidden_b_low, first=[up], second=[gate])
    finish(gate)
    weight_gate = gate.buffer.reshape(feature_width, quarter)

    def both_cores(value):
        return jnp.concatenate([value, swap(value, CORE)], axis=0)

    def forward(hidden_rows):
        gate_value = dot_plain(hidden_rows, weight_gate)
        up_value = dot_plain(hidden_rows, weight_up)
        sigmoid_gate = jax.nn.sigmoid(gate_value)
        silu_gate = gate_value * sigmoid_gate
        slope = up_value * (sigmoid_gate * (1.0 + gate_value * (1.0 - sigmoid_gate)))
        active = (silu_gate * up_value).astype(jnp.bfloat16)
        return active, silu_gate.astype(jnp.bfloat16), slope.astype(jnp.bfloat16)

    half_rows = row_total // 2
    hidden_side = [swap(hidden_b_low[:half_rows], SIDE)]
    hidden_near = both_cores(hidden_b_low)
    cot_near = both_cores(cot_low)
    cot_far = both_cores(jnp.concatenate([cot_first_other, cot_last_other], axis=0))
    hidden_near, cot_near, cot_far, hidden_b_low, *hidden_side = advance(
        [], hidden_near, cot_near, cot_far, hidden_b_low, *hidden_side,
        first=[down_a, down_b], second=[up],
    )
    finish(up)
    weight_up = up.buffer.reshape(feature_width, quarter)
    hidden_side.append(swap(hidden_b_low[half_rows:], SIDE))
    active_near, silu_near, slope_near = forward(hidden_near)
    grad_down_near = dot_first(active_near, cot_near)
    active_near, silu_near, slope_near, grad_down_near, *hidden_side = advance(
        [], active_near, silu_near, slope_near, grad_down_near, *hidden_side,
        second=[down_a, down_b],
    )
    finish(down_a, down_b)
    weight_down = jnp.concatenate(
        [down_a.buffer.reshape(quarter, down_half), down_b.buffer.reshape(quarter, down_half)], axis=1
    )

    hidden_far = both_cores(jnp.concatenate(hidden_side, axis=0))
    active_far, silu_far, slope_far = forward(hidden_far)

    def split(gradient, rows):
        return gradient.astype(jnp.bfloat16).reshape((2,) * len(zx) + rows)

    grad_down = split(grad_down_near + dot_first(active_far, cot_far), (-1, feature_width))
    grad_down, hidden_far, active_far, silu_far, slope_far = tie(
        grad_down, hidden_far, active_far, silu_far, slope_far
    )
    grad_down_a = Scatter(grad_down[..., :down_half], zx[::-1], zx, down_rank)
    grad_down_b = Scatter(grad_down[..., down_half:], zx_turned[::-1], zx, down_rank)

    def backward(cot_rows, silu_gate, slope):
        d_active = dot_second(cot_rows, weight_down)
        d_up = (d_active * silu_gate.astype(jnp.float32)).astype(jnp.bfloat16)
        d_gate = (d_active * slope.astype(jnp.float32)).astype(jnp.bfloat16)
        return d_gate, d_up

    def terms_of(parts):
        def rows(at):
            return sum(dot(left[at], right) for dot, left, right in parts)

        return rows(slice(0, row_total)), rows(slice(row_total, None)).astype(jnp.bfloat16)

    def one_core(kept, sent):
        return kept + swap(sent, CORE).astype(jnp.float32)

    d_gate_far, d_up_far = backward(cot_far, silu_far, slope_far)
    d_hidden_far = one_core(
        *terms_of([(dot_second, d_gate_far, weight_gate), (dot_second, d_up_far, weight_up)])
    ).astype(jnp.bfloat16)
    (
        d_hidden_far, d_gate_far, d_up_far, cot_near, active_far, active_near,
        grad_down_a.buffer, grad_down_b.buffer,
    ) = tie(
        d_hidden_far, d_gate_far, d_up_far, cot_near, active_far, active_near,
        grad_down_a.buffer, grad_down_b.buffer,
    )
    d_hidden_side = swap(d_hidden_far, SIDE)
    d_gate_near, d_up_near = backward(cot_near, silu_near, slope_near)
    d_hidden_kept, d_hidden_sent = terms_of(
        [(dot_second, d_gate_near, weight_gate), (dot_second, d_up_near, weight_up)]
    )
    gate_rows = (2, 2, own_rows, quarter)
    grad_gate = Scatter(
        split(dot_first(hidden_near, d_gate_near) + dot_first(hidden_far, d_gate_far), gate_rows),
        zx_turned[::-1],
        zx + group,
    )
    out_kept, out_sent = terms_of([(dot_plain, active_far, weight_down)])
    (
        d_hidden_kept, d_hidden_sent, d_hidden_side, out_kept, out_sent, d_up_near, d_up_far,
        active_near, grad_gate.buffer,
    ) = advance(
        [grad_down_a, grad_down_b],
        d_hidden_kept, d_hidden_sent, d_hidden_side, out_kept, out_sent, d_up_near, d_up_far,
        active_near, grad_gate.buffer,
    )

    out_side = swap(one_core(out_kept, out_sent).astype(jnp.bfloat16), SIDE)
    d_hidden_b = one_core(d_hidden_kept, d_hidden_sent) + d_hidden_side.astype(jnp.float32)
    d_norm_input, grad_gain_two = norm_back(d_hidden_b, normed_b, scale_b, gain_two)
    d_after = cot_full + d_norm_input
    d_branch = d_after.astype(jnp.bfloat16)
    d_gated = dot_second(d_branch, weight_out)
    d_c = (d_gated * convolved).astype(jnp.bfloat16)
    d_conv = (d_gated * c_part).reshape(seq_count, local_rows, feature_width)
    padded_grad = jnp.pad(d_conv, ((0, 0), (tap_count - 1, tap_count - 1), (0, 0)))
    span = local_rows + tap_count - 1
    d_extended = tap_values[0] * padded_grad[:, tap_count - 1 : tap_count - 1 + span]
    for offset in range(1, tap_count):
        start_at = tap_count - 1 - offset
        d_extended = d_extended + tap_values[offset] * padded_grad[:, start_at : start_at + span]
    edge_terms = d_extended[:, : tap_count - 1, :]
    grad_up = Scatter(
        split(dot_first(hidden_near, d_up_near) + dot_first(hidden_far, d_up_far), gate_rows),
        zx_turned[::-1],
        zx + group,
    )
    edge_terms, grad_up.buffer, out_side, d_branch, d_c, d_conv, active_near = advance(
        [grad_gate, grad_down_a, grad_down_b],
        edge_terms, grad_up.buffer, out_side, d_branch, d_c, d_conv, active_near,
    )

    incoming = shifted(edge_terms, "seq", -1)
    held_all = route_a + [CORE]
    shape_all = (2,) * len(held_all) + (own_rows, half_width)
    shape_one = (2,) * len(held_all) + (own_rows, feature_width)
    grad_out = Scatter(
        dot_first(gated, d_branch).astype(jnp.bfloat16).reshape(shape_one), [CORE, None], held_all
    )
    grad_c = Scatter(
        dot_first(hidden_low, d_c).astype(jnp.bfloat16).reshape(shape_one), [CORE, None], held_all
    )
    incoming_full = jnp.pad(incoming, ((0, 0), (local_rows - (tap_count - 1), 0), (0, 0)))
    d_mixed = (d_extended[:, tap_count - 1 :, :] + incoming_full).reshape(row_total, feature_width)
    d_bv = jnp.concatenate(
        [(d_mixed * v_part).astype(jnp.bfloat16), (d_mixed * b_part).astype(jnp.bfloat16)], axis=1
    )
    grad_a = Scatter(
        dot_first(hidden_low, d_bv).astype(jnp.bfloat16).reshape(shape_all),
        [CORE] + route_a[::-1],
        held_all,
    )
    d_bv, d_c, d_conv, grad_a.buffer, grad_out.buffer, grad_c.buffer = advance(
        [grad_up, grad_gate, grad_down_a, grad_down_b],
        d_bv, d_c, d_conv, grad_a.buffer, grad_out.buffer, grad_c.buffer,
    )
    finish(grad_down_a, grad_down_b)
    down_owned = jnp.concatenate([grad_down_a.buffer, grad_down_b.buffer], axis=-1)
    down_owned = quarter_owner_swap(down_owned.astype(jnp.bfloat16))
    d_hidden = dot_second(d_bv, weight_bv) + dot_second(d_c, weight_c)
    d_hidden, down_owned, grad_up.buffer, grad_gate.buffer = advance(
        [grad_a, grad_out, grad_c], d_hidden, down_owned, grad_up.buffer, grad_gate.buffer
    )
    grad_b = Scatter(
        jnp.concatenate([grad_out.buffer, grad_c.buffer], axis=-1), route_b[::-1], route_b
    )

    grad_taps = jnp.stack(
        [
            jnp.sum(d_conv * extended[:, offset : offset + local_rows], axis=(0, 1))
            for offset in range(tap_count)
        ],
        axis=0,
    )
    d_first_norm, grad_gain_one = norm_back(d_hidden, normed_a, scale_a, gain_one)
    grad_tokens = (d_after + d_first_norm).reshape(seq_count, local_rows, feature_width)
    small_terms = jnp.concatenate(
        [grad_gain_one[None, :], grad_gain_two[None, :], grad_taps], axis=0
    )

    small_terms, grad_tokens, active_near, out_side = advance(
        [grad_a, grad_b, grad_up, grad_gate], small_terms, grad_tokens, active_near, out_side
    )
    finish(grad_gate)

    def owned_quarters(cores):
        both = jnp.stack(ordered(core, *cores), axis=1)
        mine = lax.dynamic_index_in_dim(both, side, 0, keepdims=False)
        send = lax.dynamic_index_in_dim(both, 1 - side, 0, keepdims=False)
        other = swap(send.astype(jnp.bfloat16), SIDE).astype(jnp.float32)
        low, high = ordered(side, mine, other)
        return jnp.concatenate([low[0], high[0], low[1], high[1]], axis=-1)

    def summed(values, dims):
        for dim in dims:
            values = values + swap(values, dim)
        return values

    gate_core = regroup(grad_gate.buffer, 0, core, CORE)
    small_terms = summed(small_terms, [CORE] + near)
    out_own = one_core(*terms_of([(dot_plain, active_near, weight_down)]))
    results = after_mix + (out_own + out_side.astype(jnp.float32))
    block_out = results.astype(jnp.bfloat16).reshape(seq_count, local_rows, feature_width)
    small_terms, block_out, *gate_core = advance(
        [grad_a, grad_b, grad_up], small_terms, block_out, *gate_core
    )
    finish(grad_up)
    gate_owned = owned_quarters(gate_core)
    up_core = regroup(grad_up.buffer, 0, core, CORE)
    small_terms = summed(small_terms, [SIDE] + outer + far[:-1])
    small_terms, gate_owned, *up_core = advance([grad_a, grad_b], small_terms, gate_owned, *up_core)
    up_owned = owned_quarters(up_core)
    small_terms = summed(small_terms, far[-1:])
    finish(grad_a, grad_b)
    owned_a, owned_b = grad_a.buffer, grad_b.buffer
    place = lax.axis_index("fsdp") * lax.axis_size("seq") + lax.axis_index("seq")
    small_owned = lax.dynamic_slice_in_dim(small_terms, place * own_rows, own_rows, axis=1)
    return (
        block_out,
        grad_tokens,
        small_owned[0],
        jnp.concatenate(
            [owned_a[:, :feature_width], owned_b[:, feature_width:], owned_a[:, feature_width:]],
            axis=1,
        ),
        small_owned[2:],
        owned_b[:, :feature_width],
        small_owned[1],
        gate_owned,
        up_owned,
        down_owned.astype(jnp.float32),
    )


def solution(mesh):
    return jax.shard_map(
        body,
        mesh=mesh,
        in_specs=(
            P("fsdp", "seq", None),
            P(("fsdp", "seq")),
            P(("fsdp", "seq"), None),
            P(None, ("fsdp", "seq")),
            P(("fsdp", "seq"), None),
            P(("fsdp", "seq")),
            P(("fsdp", "seq"), None),
            P(("fsdp", "seq"), None),
            P(("fsdp", "seq"), None),
            P("fsdp", "seq", None),
        ),
        out_specs=(
            P("fsdp", "seq", None),
            P("fsdp", "seq", None),
            P(("fsdp", "seq")),
            P(("fsdp", "seq"), None),
            P(None, ("fsdp", "seq")),
            P(("fsdp", "seq"), None),
            P(("fsdp", "seq")),
            P(("fsdp", "seq"), None),
            P(("fsdp", "seq"), None),
            P(("fsdp", "seq"), None),
        ),
        check_vma=False,
    )
```

```python
import jax
import jax.numpy as jnp
from jax import lax
from jax.sharding import PartitionSpec as P

EPSILON = 1e-05
CORE = ("fsdp", 0)
SIDE = ("seq", 0)
WAY = ("way", 0)


def shifted(shard, axis, by):
    size = lax.axis_size(axis)
    pairs = [(i, i + by) for i in range(size) if 0 <= i + by < size]
    return lax.ppermute(shard, axis, pairs)


def bit_count(axis):
    return lax.axis_size(axis).bit_length() - 1


def my_bit(dim):
    axis, bit = dim
    return (lax.axis_index(axis) >> bit) & 1


def swap(value, dim):
    axis, bit = dim
    return lax.ppermute(value, axis, [(i, i ^ (1 << bit)) for i in range(lax.axis_size(axis))])


def rank(dim):
    axis, bit = dim
    return (0 if axis == "fsdp" else 1, -bit)


def down_rank(dim):
    top = bit_count("fsdp") - 1
    return rank({("fsdp", top): CORE, ("fsdp", top - 1): SIDE}.get(dim, dim))


def tie(*values):
    return lax.optimization_barrier(values)


class Chain:
    def __init__(self, dims, held, order):
        self.left, self.held, self.order = list(dims), list(held), order
        self.parts, self.ready = [], []

    def prepare(self):
        self.ready = [self.sent()]

    def start(self):
        if self.left:
            sent = self.ready.pop() if self.ready else self.sent()
            self.parts = [swap(sent, self.left[0])]

    def start_half(self, half):
        if self.left:
            sent = self.sent()
            middle = sent.shape[0] // 2
            part = swap(sent[middle:] if half else sent[:middle], self.left[0])
            self.parts = self.parts + [part] if half else [part]

    def merge(self):
        if self.left:
            other = self.parts[0] if len(self.parts) == 1 else jnp.concatenate(self.parts, axis=0)
            self.parts = []
            self.take(self.left.pop(0), other)


class Gather(Chain):
    def __init__(self, piece, dims, held=(), order=rank):
        super().__init__(dims, held, order)
        self.arrays = [piece]

    def value(self):
        return self.arrays[0]

    def sent(self):
        return self.arrays[0]

    def take(self, dim, other):
        axis = sum(self.order(h) < self.order(dim) for h in self.held)
        high, mine = my_bit(dim) == 1, self.arrays[0]
        self.arrays = [
            jnp.stack([jnp.where(high, other, mine), jnp.where(high, mine, other)], axis=axis)
        ]
        self.held.append(dim)


class Scatter(Chain):
    def __init__(self, terms, dims, held, order=rank):
        super().__init__(dims, sorted(held, key=order), order)
        self.arrays, self.cuts = [terms], [[]]

    def summed(self, further):
        total = 0.0
        for array, cuts in zip(self.arrays, self.cuts):
            for axis, index in cuts + further:
                array = lax.dynamic_index_in_dim(array, index, axis, keepdims=False)
            total = total + array.astype(jnp.float32)
        return total

    def value(self):
        return self.summed([])

    def sent(self):
        dim = self.left[0]
        return self.summed([(self.held.index(dim), 1 - my_bit(dim))]).astype(jnp.bfloat16)

    def take(self, dim, other):
        cut = (self.held.index(dim), my_bit(dim))
        self.cuts = [cuts + [cut] for cuts in self.cuts] + [[]]
        self.arrays = self.arrays + [other]
        self.held.remove(dim)


class Joint(Chain):
    def __init__(self, chains, axis):
        super().__init__(chains[0].left, chains[0].held, chains[0].order)
        self.chains, self.axis = chains, axis

    @property
    def arrays(self):
        return [array for chain in self.chains for array in chain.arrays]

    @arrays.setter
    def arrays(self, values):
        for chain in self.chains:
            chain.arrays, values = values[: len(chain.arrays)], values[len(chain.arrays) :]

    def sent(self):
        return jnp.concatenate([chain.sent() for chain in self.chains], axis=self.axis)

    def take(self, dim, other):
        for chain, part in zip(self.chains, jnp.split(other, len(self.chains), axis=self.axis)):
            chain.left.pop(0)
            chain.take(dim, part)

    def value(self):
        return jnp.concatenate([chain.value() for chain in self.chains], axis=self.axis)


def tie_chains(chains, *others, parts=True):
    flat = [array for chain in chains for array in chain.arrays]
    flat += [array for chain in chains for array in chain.ready]
    if parts:
        flat += [part for chain in chains for part in chain.parts]
    tied = list(tie(*flat, *others))
    for chain in chains:
        chain.arrays = [tied.pop(0) for _ in chain.arrays]
    for chain in chains:
        chain.ready = [tied.pop(0) for _ in chain.ready]
    for chain in chains if parts else ():
        chain.parts = [tied.pop(0) for _ in chain.parts]
    return tied


def advance(chains, *others, first=(), second=()):
    for chain in chains:
        chain.start()
    for chain in first:
        chain.start_half(0)
    for chain in second:
        chain.start_half(1)
    every = [*chains, *first, *second]
    others = tie_chains(every, *others, parts=False)
    for chain in [*chains, *second]:
        chain.merge()
    return tie_chains(every, *others)


def step(chain):
    chain.start()
    chain.merge()


def joint(chains, axis):
    for chain in chains:
        while chain.left[:1] != chains[0].left[-1:]:
            step(chain)
    return Joint(chains, axis)


def finish(*chains):
    for chain in chains:
        while chain.left:
            step(chain)


def normalize(values, gain):
    scale = lax.rsqrt(jnp.mean(values * values, axis=-1, keepdims=True) + EPSILON)
    normalized_rows = values * scale
    return (normalized_rows, scale, normalized_rows * gain)


def norm_back(d_hidden, normalized_rows, scale, gain):
    norm_gradient = d_hidden * gain
    grad_gain = jnp.sum(d_hidden * normalized_rows, axis=0)
    d_input = scale * (
        norm_gradient
        - normalized_rows * jnp.mean(norm_gradient * normalized_rows, axis=-1, keepdims=True)
    )
    return (d_input, grad_gain)


def dot_plain(left_segment, right_segment):
    return jnp.dot(left_segment, right_segment, preferred_element_type=jnp.float32)


def dot_first(left_segment, right_segment):
    return lax.dot_general(
        left_segment, right_segment, (((0,), (0,)), ((), ())), preferred_element_type=jnp.float32
    )


def dot_second(left_segment, right_segment):
    return lax.dot_general(
        left_segment, right_segment, (((1,), (1,)), ((), ())), preferred_element_type=jnp.float32
    )


def quarter_owner_swap(value):
    fsdp, seq = lax.axis_size("fsdp"), lax.axis_size("seq")
    top = bit_count("fsdp") - 1
    pairs = []
    for device in range(fsdp * seq):
        f, s = divmod(device, seq)
        high, low = (f >> top) & 1, (f >> (top - 1)) & 1
        core, side = f & 1, s & 1
        f2 = (f & ~((1 << top) | (1 << (top - 1)) | 1)) | (core << top) | (side << (top - 1)) | high
        pairs.append((device, f2 * seq + ((s & ~1) | low)))
    return lax.ppermute(value, ("fsdp", "seq"), pairs)


def body(tokens, gain_a, mix_in, conv_tap, mix_out, gain_b, ff_gate, ff_up, ff_down, cotangent):
    seq_count, local_rows, feature_width = tokens.shape
    row_total = seq_count * local_rows
    tap_count = conv_tap.shape[0]
    own_rows = mix_in.shape[0]
    hidden_units = ff_gate.shape[1]
    quarter = hidden_units // 4
    core, side = my_bit(CORE), my_bit(SIDE)
    near = [("fsdp", 1)]
    far = [("fsdp", b) for b in range(2, bit_count("fsdp"))]
    outer = [("seq", b) for b in range(1, bit_count("seq"))]
    zx, zx_turned = far + near + outer, far[::-1] + near + outer
    x_first, z_first = outer + near + far[:1], far[:1] + outer + near
    route_a, route_b = far + near + outer + [SIDE], far[::-1] + [SIDE] + outer + near
    group = [CORE, SIDE]
    half_width = 2 * feature_width
    down_half = feature_width // 2

    def ordered(pair_bit, mine, other):
        high = pair_bit == 1
        return jnp.where(high, other, mine), jnp.where(high, mine, other)

    small = jnp.concatenate([gain_a[None], gain_b[None], conv_tap], axis=0).T
    small = jnp.pad(small, ((0, 0), (0, 128 - small.shape[1])))
    mix_a = Gather(
        jnp.concatenate([mix_in[:, :feature_width], mix_in[:, 2 * feature_width :]], axis=1), route_a
    )
    mix_b = Gather(
        jnp.concatenate([mix_in[:, feature_width : 2 * feature_width], mix_out, small], axis=1),
        route_b,
    )
    down_piece = quarter_owner_swap(ff_down)

    def quarters(shard):
        return jnp.stack([shard[:, q * quarter : (q + 1) * quarter] for q in range(4)]).reshape(
            2, 2, own_rows, quarter
        )

    def regroup(parts, axis, bit, dim):
        mine = lax.dynamic_index_in_dim(parts, bit, axis, keepdims=False)
        other = swap(lax.dynamic_index_in_dim(parts, 1 - bit, axis, keepdims=False), dim)
        return mine, other

    gate_mine, gate_other = regroup(quarters(ff_gate), 1, side, SIDE)
    up_mine, up_other = regroup(quarters(ff_up), 1, side, SIDE)
    cot_low = cotangent.reshape(row_total, feature_width)
    cot_first, cot_last = cot_low[: row_total // 2], cot_low[row_total // 2 :]
    gate_mine, gate_other, up_mine, up_other, cot_first, down_piece = advance(
        [mix_a, mix_b], gate_mine, gate_other, up_mine, up_other, cot_first, down_piece
    )
    down_x = Gather(down_piece, near + outer, (), down_rank)

    def regroup_core(mine, other):
        both = jnp.stack(ordered(side, mine, other), axis=1)
        return jnp.stack(ordered(core, *regroup(both, 0, core, CORE)), axis=0)

    gate = Gather(regroup_core(gate_mine, gate_other), zx_turned, group)
    up = Gather(regroup_core(up_mine, up_other), zx, group)
    cot_first_other = swap(cot_first, SIDE)
    cot_first_other, cot_last = advance([mix_a, mix_b, down_x], cot_first_other, cot_last)
    tie_chains([gate, up, mix_a, mix_b])

    finish(down_x)
    while mix_a.left or mix_b.left:
        down_piece, cot_last = advance([mix_a, mix_b, gate, up], down_x.value(), cot_last)

    inputs = tokens.reshape(row_total, feature_width).astype(jnp.float32)
    cot_full = cot_low.astype(jnp.float32)
    cot_last_other = swap(cot_last, SIDE)
    core_a, core_b = Gather(mix_a.value(), [CORE], mix_a.held), Gather(mix_b.value(), [CORE], mix_b.held)
    step(core_a)
    step(core_b)
    weight_bv = core_a.value().reshape(feature_width, half_width)
    weight_c_out = core_b.value().reshape(feature_width, half_width + 128)
    weight_c = weight_c_out[:, :feature_width]
    weight_out = weight_c_out[:, feature_width:half_width]
    small_whole = weight_c_out[:, half_width : half_width + 2 + tap_count].T.astype(jnp.float32)
    gain_one, gain_two, tap_values = small_whole[0], small_whole[1], small_whole[2:]
    normed_a, scale_a, hidden = normalize(inputs, gain_one)
    hidden_low = hidden.astype(jnp.bfloat16)
    bv_part = dot_plain(hidden_low, weight_bv)
    b_part = bv_part[:, :feature_width]
    v_part = bv_part[:, feature_width:]
    mixed = (b_part * v_part).astype(jnp.bfloat16).reshape(seq_count, local_rows, feature_width)
    mixed, hidden_low, weight_c, down_piece, cot_last_other = advance(
        [], mixed, hidden_low, weight_c, down_piece, cot_last_other, first=[gate]
    )
    edge_rows = shifted(mixed[:, local_rows - (tap_count - 1) :, :], "seq", 1)
    c_part = dot_plain(hidden_low, weight_c)
    extended = jnp.concatenate([edge_rows, mixed], axis=1).astype(jnp.float32)
    convolved = tap_values[0] * extended[:, 0:local_rows]
    for offset in range(1, tap_count):
        convolved = convolved + tap_values[offset] * extended[:, offset : offset + local_rows]
    convolved = convolved.reshape(row_total, feature_width)
    gated = (c_part * convolved).astype(jnp.bfloat16)
    after_mix = inputs + dot_plain(gated, weight_out)
    normed_b, scale_b, hidden_b = normalize(after_mix, gain_two)
    hidden_b_low = hidden_b.astype(jnp.bfloat16)
    down_a = Gather(down_piece[..., :down_half], far, near + outer, down_rank)
    down_b = Gather(down_piece[..., down_half:], far[::-1], near + outer, down_rank)
    (hidden_b_low,) = advance([down_a, down_b], hidden_b_low, first=[up], second=[gate])
    finish(gate)
    weight_gate = gate.value().reshape(feature_width, quarter)

    def both_cores(value):
        return jnp.concatenate([value, swap(value, CORE)], axis=0)

    def forward(hidden_rows):
        gate_value = dot_plain(hidden_rows, weight_gate)
        up_value = dot_plain(hidden_rows, weight_up)
        sigmoid_gate = jax.nn.sigmoid(gate_value)
        silu_gate = gate_value * sigmoid_gate
        slope = up_value * (sigmoid_gate * (1.0 + gate_value * (1.0 - sigmoid_gate)))
        active = (silu_gate * up_value).astype(jnp.bfloat16)
        return active, silu_gate.astype(jnp.bfloat16), slope.astype(jnp.bfloat16)

    half_rows = row_total // 2
    hidden_side = [swap(hidden_b_low[:half_rows], SIDE)]
    hidden_near = both_cores(hidden_b_low)
    cot_near = both_cores(cot_low)
    cot_far = both_cores(jnp.concatenate([cot_first_other, cot_last_other], axis=0))
    hidden_near, cot_near, cot_far, hidden_b_low, *hidden_side = advance(
        [], hidden_near, cot_near, cot_far, hidden_b_low, *hidden_side,
        first=[down_a, down_b], second=[up],
    )
    finish(up)
    weight_up = up.value().reshape(feature_width, quarter)
    hidden_side.append(swap(hidden_b_low[half_rows:], SIDE))
    active_near, silu_near, slope_near = forward(hidden_near)
    grad_down_near = dot_first(active_near, cot_near)
    active_near, silu_near, slope_near, grad_down_near, *hidden_side = advance(
        [], active_near, silu_near, slope_near, grad_down_near, *hidden_side,
        second=[down_a, down_b],
    )
    finish(down_a, down_b)
    weight_down = jnp.concatenate(
        [down_a.value().reshape(quarter, down_half), down_b.value().reshape(quarter, down_half)], axis=1
    )

    hidden_far = both_cores(jnp.concatenate(hidden_side, axis=0))
    active_far, silu_far, slope_far = forward(hidden_far)

    def split(gradient, rows):
        return gradient.astype(jnp.bfloat16).reshape((2,) * len(zx) + rows)

    grad_down = split(grad_down_near + dot_first(active_far, cot_far), (-1, feature_width))
    grad_down, hidden_far, active_far, silu_far, slope_far = tie(
        grad_down, hidden_far, active_far, silu_far, slope_far
    )
    grad_down_a = Scatter(grad_down[..., :down_half], x_first + far[1:], zx, down_rank)
    grad_down_b = Scatter(grad_down[..., down_half:], z_first + far[1:], zx, down_rank)

    def backward(cot_rows, silu_gate, slope):
        d_active = dot_second(cot_rows, weight_down)
        d_up = (d_active * silu_gate.astype(jnp.float32)).astype(jnp.bfloat16)
        d_gate = (d_active * slope.astype(jnp.float32)).astype(jnp.bfloat16)
        return d_gate, d_up

    def terms_of(parts):
        def rows(at):
            return sum(dot(left[at], right) for dot, left, right in parts)

        return rows(slice(0, row_total)), rows(slice(row_total, None)).astype(jnp.bfloat16)

    def one_core(kept, sent):
        return kept + swap(sent, CORE).astype(jnp.float32)

    d_gate_far, d_up_far = backward(cot_far, silu_far, slope_far)
    d_hidden_far = one_core(
        *terms_of([(dot_second, d_gate_far, weight_gate), (dot_second, d_up_far, weight_up)])
    ).astype(jnp.bfloat16)
    out_kept, out_sent = terms_of([(dot_plain, active_far, weight_down)])
    d_hidden_far, d_gate_far, d_up_far, cot_near, out_kept, out_sent, active_near = tie_chains(
        [grad_down_a, grad_down_b],
        d_hidden_far, d_gate_far, d_up_far, cot_near, out_kept, out_sent, active_near,
    )
    d_hidden_side = [swap(d_hidden_far[:half_rows], SIDE)]
    d_gate_near, d_up_near = backward(cot_near, silu_near, slope_near)
    d_hidden_kept, d_hidden_sent = terms_of(
        [(dot_second, d_gate_near, weight_gate), (dot_second, d_up_near, weight_up)]
    )
    (
        d_hidden_kept, d_hidden_sent, d_hidden_far, d_gate_near, d_gate_far, d_up_near, d_up_far,
        out_kept, out_sent, active_near, *d_hidden_side,
    ) = advance(
        [grad_down_a, grad_down_b],
        d_hidden_kept, d_hidden_sent, d_hidden_far, d_gate_near, d_gate_far, d_up_near, d_up_far,
        out_kept, out_sent, active_near, *d_hidden_side,
    )
    d_hidden_side.append(swap(d_hidden_far[half_rows:], SIDE))
    gate_rows = (2, 2, own_rows, quarter)

    def two_scatters(near_terms, far_terms):
        terms = split(
            dot_first(hidden_near, near_terms) + dot_first(hidden_far, far_terms), gate_rows
        )
        return [
            Scatter(
                lax.index_in_dim(terms, way, len(far) + 1, keepdims=False), dims + far[1:], zx + [SIDE]
            )
            for way, dims in enumerate((x_first, z_first))
        ]

    grad_gate = two_scatters(d_gate_near, d_gate_far)
    out_received = swap(out_sent, CORE)
    (
        d_hidden_kept, d_hidden_sent, out_kept, out_received, d_up_near, d_up_far, active_near,
        *d_hidden_side,
    ) = advance(
        [grad_down_a, grad_down_b],
        d_hidden_kept, d_hidden_sent, out_kept, out_received, d_up_near, d_up_far, active_near,
        *d_hidden_side,
    )
    grad_down = joint([grad_down_a, grad_down_b], -1)
    out_far = (out_kept + out_received.astype(jnp.float32)).astype(jnp.bfloat16)
    out_far, *d_hidden_side = tie_chains([grad_down, *grad_gate], out_far, *d_hidden_side)
    d_hidden_side = jnp.concatenate(d_hidden_side, axis=0)

    out_side = swap(out_far, SIDE)
    d_hidden_b = one_core(d_hidden_kept, d_hidden_sent) + d_hidden_side.astype(jnp.float32)
    d_norm_input, grad_gain_two = norm_back(d_hidden_b, normed_b, scale_b, gain_two)
    d_after = cot_full + d_norm_input
    d_branch = d_after.astype(jnp.bfloat16)
    d_gated = dot_second(d_branch, weight_out)
    d_c = (d_gated * convolved).astype(jnp.bfloat16)
    d_conv = (d_gated * c_part).reshape(seq_count, local_rows, feature_width)
    padded_grad = jnp.pad(d_conv, ((0, 0), (tap_count - 1, tap_count - 1), (0, 0)))
    span = local_rows + tap_count - 1
    d_extended = tap_values[0] * padded_grad[:, tap_count - 1 : tap_count - 1 + span]
    for offset in range(1, tap_count):
        start_at = tap_count - 1 - offset
        d_extended = d_extended + tap_values[offset] * padded_grad[:, start_at : start_at + span]
    edge_terms = d_extended[:, : tap_count - 1, :]
    grad_up = two_scatters(d_up_near, d_up_far)
    held_all = route_a + [CORE]
    shape_all = (2,) * len(held_all) + (own_rows, half_width)
    shape_one = (2,) * len(held_all) + (own_rows, feature_width)
    (
        edge_terms, out_side, d_branch, d_c, d_conv, active_near,
    ) = advance(
        [*grad_gate, grad_down],
        edge_terms, out_side, d_branch, d_c, d_conv, active_near,
    )
    finish(grad_down)
    down_owned, *_ = tie_chains([*grad_gate, *grad_up], grad_down.value().astype(jnp.bfloat16))

    incoming = shifted(edge_terms, "seq", -1)
    grad_out = Scatter(
        dot_first(gated, d_branch).astype(jnp.bfloat16).reshape(shape_one), [CORE] + route_b[::-1], held_all
    )
    grad_c = Scatter(
        dot_first(hidden_low, d_c).astype(jnp.bfloat16).reshape(shape_one), [CORE] + route_b[::-1], held_all
    )
    incoming_full = jnp.pad(incoming, ((0, 0), (local_rows - (tap_count - 1), 0), (0, 0)))
    d_mixed = (d_extended[:, tap_count - 1 :, :] + incoming_full).reshape(row_total, feature_width)
    d_bv = jnp.concatenate(
        [(d_mixed * v_part).astype(jnp.bfloat16), (d_mixed * b_part).astype(jnp.bfloat16)], axis=1
    )
    grad_a = Scatter(
        dot_first(hidden_low, d_bv).astype(jnp.bfloat16).reshape(shape_all),
        [CORE] + route_a[::-1],
        held_all,
    )
    d_bv, d_c, d_conv, out_side, down_owned = advance(
        [*grad_up, *grad_gate], d_bv, d_c, d_conv, out_side, down_owned
    )

    grad_gate = joint(grad_gate, 0)
    grad_gate.prepare()
    for chain in grad_up:
        chain.prepare()
    down_owned = quarter_owner_swap(down_owned)
    d_hidden = dot_second(d_bv, weight_bv) + dot_second(d_c, weight_c)
    d_hidden, down_owned = advance([grad_a, grad_out, grad_c], d_hidden, down_owned)
    grad_b = Joint([grad_out, grad_c], -1)
    tie_chains([grad_b, grad_a, grad_gate, *grad_up])

    grad_taps = jnp.stack(
        [
            jnp.sum(d_conv * extended[:, offset : offset + local_rows], axis=(0, 1))
            for offset in range(tap_count)
        ],
        axis=0,
    )
    d_first_norm, grad_gain_one = norm_back(d_hidden, normed_a, scale_a, gain_one)
    grad_tokens = (d_after + d_first_norm).reshape(seq_count, local_rows, feature_width)
    small_terms = jnp.concatenate(
        [grad_gain_one[None, :], grad_gain_two[None, :], grad_taps], axis=0
    )

    small_terms, grad_tokens, active_near = advance(
        [grad_a, grad_b, *grad_up, grad_gate], small_terms, grad_tokens, active_near
    )
    finish(grad_gate)
    grad_up = joint(grad_up, 0)

    def owned_rows(joint_chain):
        return jnp.stack([chain.value() for chain in joint_chain.chains])

    def owned_quarters(cores):
        both = jnp.stack(ordered(core, *cores), axis=1)
        mine = lax.dynamic_index_in_dim(both, side, 0, keepdims=False)
        send = lax.dynamic_index_in_dim(both, 1 - side, 0, keepdims=False)
        other = swap(send.astype(jnp.bfloat16), SIDE).astype(jnp.float32)
        low, high = ordered(side, mine, other)
        return jnp.concatenate([low[0], high[0], low[1], high[1]], axis=-1)

    small_terms = small_terms + swap(small_terms, CORE)
    out_own = one_core(*terms_of([(dot_plain, active_near, weight_down)]))
    gate_core = regroup(owned_rows(grad_gate), 0, core, CORE)
    small_terms, out_own, *gate_core = advance(
        [grad_a, grad_b, grad_up], small_terms, out_own, *gate_core
    )
    finish(grad_up)
    gate_owned = owned_quarters(gate_core)
    up_core = regroup(owned_rows(grad_up), 0, core, CORE)
    for dim in near + [SIDE] + outer:
        small_terms = small_terms + swap(small_terms, dim)
    small_terms, gate_owned, *up_core = advance(
        [grad_a, grad_b], small_terms, gate_owned, *up_core
    )
    up_owned = owned_quarters(up_core)
    results = after_mix + (out_own + out_side.astype(jnp.float32))
    block_out = results.astype(jnp.bfloat16).reshape(seq_count, local_rows, feature_width)
    up_owned = owned_quarters(up_core)
    for dim in far:
        small_terms = small_terms + swap(small_terms, dim)
    finish(grad_a, grad_b)
    owned_a, owned_b = grad_a.value(), grad_b.value()
    place = lax.axis_index("fsdp") * lax.axis_size("seq") + lax.axis_index("seq")
    small_owned = lax.dynamic_slice_in_dim(small_terms, place * own_rows, own_rows, axis=1)
    return (
        block_out,
        grad_tokens,
        small_owned[0],
        jnp.concatenate(
            [owned_a[:, :feature_width], owned_b[:, feature_width:], owned_a[:, feature_width:]],
            axis=1,
        ),
        small_owned[2:],
        owned_b[:, :feature_width],
        small_owned[1],
        gate_owned,
        up_owned,
        down_owned.astype(jnp.float32),
    )


def solution(mesh):
    return jax.shard_map(
        body,
        mesh=mesh,
        in_specs=(
            P("fsdp", "seq", None),
            P(("fsdp", "seq")),
            P(("fsdp", "seq"), None),
            P(None, ("fsdp", "seq")),
            P(("fsdp", "seq"), None),
            P(("fsdp", "seq")),
            P(("fsdp", "seq"), None),
            P(("fsdp", "seq"), None),
            P(("fsdp", "seq"), None),
            P("fsdp", "seq", None),
        ),
        out_specs=(
            P("fsdp", "seq", None),
            P("fsdp", "seq", None),
            P(("fsdp", "seq")),
            P(("fsdp", "seq"), None),
            P(None, ("fsdp", "seq")),
            P(("fsdp", "seq"), None),
            P(("fsdp", "seq")),
            P(("fsdp", "seq"), None),
            P(("fsdp", "seq"), None),
            P(("fsdp", "seq"), None),
        ),
        check_vma=False,
    )
```

```python
import jax
import jax.numpy as jnp
from jax import lax
from jax.sharding import PartitionSpec as P

EPSILON = 1e-05
CORE = ("fsdp", 0)
SIDE = ("seq", 0)
WAY = ("way", 0)


def shifted(shard, axis, by):
    size = lax.axis_size(axis)
    pairs = [(i, i + by) for i in range(size) if 0 <= i + by < size]
    return lax.ppermute(shard, axis, pairs)


def bit_count(axis):
    return lax.axis_size(axis).bit_length() - 1


def my_bit(dim):
    axis, bit = dim
    return (lax.axis_index(axis) >> bit) & 1


def swap(value, dim):
    axis, bit = dim
    return lax.ppermute(value, axis, [(i, i ^ (1 << bit)) for i in range(lax.axis_size(axis))])


def rank(dim):
    axis, bit = dim
    return (0 if axis == "fsdp" else 1, -bit)


def down_rank(dim):
    top = bit_count("fsdp") - 1
    return rank({("fsdp", top): CORE, ("fsdp", top - 1): SIDE}.get(dim, dim))


def tie(*values):
    return lax.optimization_barrier(values)


class Chain:
    def __init__(self, dims, held, order):
        self.left, self.held, self.order = list(dims), list(held), order
        self.parts, self.ready = [], []

    def prepare(self):
        self.ready = [self.sent()]

    def start(self):
        if self.left:
            sent = self.ready.pop() if self.ready else self.sent()
            self.parts = [swap(sent, self.left[0])]

    def start_half(self, half):
        if self.left:
            sent = self.sent()
            middle = sent.shape[0] // 2
            part = swap(sent[middle:] if half else sent[:middle], self.left[0])
            self.parts = self.parts + [part] if half else [part]

    def merge(self):
        if self.left:
            other = self.parts[0] if len(self.parts) == 1 else jnp.concatenate(self.parts, axis=0)
            self.parts = []
            self.take(self.left.pop(0), other)


class Gather(Chain):
    def __init__(self, piece, dims, held=(), order=rank):
        super().__init__(dims, held, order)
        self.arrays = [piece]

    def value(self):
        return self.arrays[0]

    def sent(self):
        return self.arrays[0]

    def take(self, dim, other):
        axis = sum(self.order(h) < self.order(dim) for h in self.held)
        high, mine = my_bit(dim) == 1, self.arrays[0]
        self.arrays = [
            jnp.stack([jnp.where(high, other, mine), jnp.where(high, mine, other)], axis=axis)
        ]
        self.held.append(dim)


class Scatter(Chain):
    def __init__(self, terms, dims, held, order=rank):
        super().__init__(dims, sorted(held, key=order), order)
        self.arrays, self.cuts = [terms], [[]]

    def summed(self, further):
        total = 0.0
        for array, cuts in zip(self.arrays, self.cuts):
            for axis, index in cuts + further:
                array = lax.dynamic_index_in_dim(array, index, axis, keepdims=False)
            total = total + array.astype(jnp.float32)
        return total

    def value(self):
        return self.summed([])

    def sent(self):
        dim = self.left[0]
        return self.summed([(self.held.index(dim), 1 - my_bit(dim))]).astype(jnp.bfloat16)

    def take(self, dim, other):
        cut = (self.held.index(dim), my_bit(dim))
        self.cuts = [cuts + [cut] for cuts in self.cuts] + [[]]
        self.arrays = self.arrays + [other]
        self.held.remove(dim)


class Joint(Chain):
    def __init__(self, chains, axis):
        super().__init__(chains[0].left, chains[0].held, chains[0].order)
        self.chains, self.axis = chains, axis

    @property
    def arrays(self):
        return [array for chain in self.chains for array in chain.arrays]

    @arrays.setter
    def arrays(self, values):
        for chain in self.chains:
            chain.arrays, values = values[: len(chain.arrays)], values[len(chain.arrays) :]

    def sent(self):
        return jnp.concatenate([chain.sent() for chain in self.chains], axis=self.axis)

    def take(self, dim, other):
        for chain, part in zip(self.chains, jnp.split(other, len(self.chains), axis=self.axis)):
            chain.left.pop(0)
            chain.take(dim, part)

    def value(self):
        return jnp.concatenate([chain.value() for chain in self.chains], axis=self.axis)


def tie_chains(chains, *others, parts=True):
    flat = [array for chain in chains for array in chain.arrays]
    flat += [array for chain in chains for array in chain.ready]
    if parts:
        flat += [part for chain in chains for part in chain.parts]
    tied = list(tie(*flat, *others))
    for chain in chains:
        chain.arrays = [tied.pop(0) for _ in chain.arrays]
    for chain in chains:
        chain.ready = [tied.pop(0) for _ in chain.ready]
    for chain in chains if parts else ():
        chain.parts = [tied.pop(0) for _ in chain.parts]
    return tied


def advance(chains, *others, first=(), second=()):
    for chain in chains:
        chain.start()
    for chain in first:
        chain.start_half(0)
    for chain in second:
        chain.start_half(1)
    every = [*chains, *first, *second]
    others = tie_chains(every, *others, parts=False)
    for chain in [*chains, *second]:
        chain.merge()
    return tie_chains(every, *others)


def step(chain):
    chain.start()
    chain.merge()


def joint(chains, axis):
    for chain in chains:
        while chain.left[:1] != chains[0].left[-1:]:
            step(chain)
    return Joint(chains, axis)


def finish(*chains):
    for chain in chains:
        while chain.left:
            step(chain)


def normalize(values, gain):
    scale = lax.rsqrt(jnp.mean(values * values, axis=-1, keepdims=True) + EPSILON)
    normalized_rows = values * scale
    return (normalized_rows, scale, normalized_rows * gain)


def norm_back(d_hidden, normalized_rows, scale, gain):
    norm_gradient = d_hidden * gain
    grad_gain = jnp.sum(d_hidden * normalized_rows, axis=0)
    d_input = scale * (
        norm_gradient
        - normalized_rows * jnp.mean(norm_gradient * normalized_rows, axis=-1, keepdims=True)
    )
    return (d_input, grad_gain)


def dot_plain(left_segment, right_segment):
    return jnp.dot(left_segment, right_segment, preferred_element_type=jnp.float32)


def dot_first(left_segment, right_segment):
    return lax.dot_general(
        left_segment, right_segment, (((0,), (0,)), ((), ())), preferred_element_type=jnp.float32
    )


def dot_second(left_segment, right_segment):
    return lax.dot_general(
        left_segment, right_segment, (((1,), (1,)), ((), ())), preferred_element_type=jnp.float32
    )


def quarter_owner_swap(value):
    fsdp, seq = lax.axis_size("fsdp"), lax.axis_size("seq")
    top = bit_count("fsdp") - 1
    pairs = []
    for device in range(fsdp * seq):
        f, s = divmod(device, seq)
        high, low = (f >> top) & 1, (f >> (top - 1)) & 1
        core, side = f & 1, s & 1
        f2 = (f & ~((1 << top) | (1 << (top - 1)) | 1)) | (core << top) | (side << (top - 1)) | high
        pairs.append((device, f2 * seq + ((s & ~1) | low)))
    return lax.ppermute(value, ("fsdp", "seq"), pairs)


def body(tokens, gain_a, mix_in, conv_tap, mix_out, gain_b, ff_gate, ff_up, ff_down, cotangent):
    seq_count, local_rows, feature_width = tokens.shape
    row_total = seq_count * local_rows
    tap_count = conv_tap.shape[0]
    own_rows = mix_in.shape[0]
    hidden_units = ff_gate.shape[1]
    quarter = hidden_units // 4
    core, side = my_bit(CORE), my_bit(SIDE)
    near = [("fsdp", 1)]
    far = [("fsdp", b) for b in range(2, bit_count("fsdp"))]
    outer = [("seq", b) for b in range(1, bit_count("seq"))]
    zx, zx_turned = far + near + outer, far[::-1] + near + outer
    x_first, z_first = outer + near + far[:1], far[:1] + outer + near
    route_a, route_b = far + near + outer + [SIDE], far[::-1] + [SIDE] + outer + near
    group = [CORE, SIDE]
    half_width = 2 * feature_width
    down_half = feature_width // 2

    def ordered(pair_bit, mine, other):
        high = pair_bit == 1
        return jnp.where(high, other, mine), jnp.where(high, mine, other)

    small = jnp.concatenate([gain_a[None], gain_b[None], conv_tap], axis=0).T
    small = jnp.pad(small, ((0, 0), (0, 128 - small.shape[1])))
    mix_a = Gather(
        jnp.concatenate([mix_in[:, :feature_width], mix_in[:, 2 * feature_width :]], axis=1), route_a
    )
    mix_b = Gather(
        jnp.concatenate([mix_in[:, feature_width : 2 * feature_width], mix_out, small], axis=1),
        route_b,
    )

    def quarters(shard):
        return jnp.stack([shard[:, q * quarter : (q + 1) * quarter] for q in range(4)]).reshape(
            2, 2, own_rows, quarter
        )

    def regroup(parts, axis, bit, dim):
        mine = lax.dynamic_index_in_dim(parts, bit, axis, keepdims=False)
        other = swap(lax.dynamic_index_in_dim(parts, 1 - bit, axis, keepdims=False), dim)
        return mine, other

    gate_up = regroup(jnp.stack([quarters(ff_gate), quarters(ff_up)]), 2, side, SIDE)
    cot_low = cotangent.reshape(row_total, feature_width)
    cot_first, cot_last = cot_low[: row_total // 2], cot_low[row_total // 2 :]
    down_piece = quarter_owner_swap(ff_down)
    *gate_up, cot_first, down_piece = advance([mix_a, mix_b], *gate_up, cot_first, down_piece)

    gate_up = regroup(jnp.stack(ordered(side, *gate_up), axis=2), 1, core, CORE)
    gate_piece, up_piece = jnp.stack(ordered(core, *gate_up), axis=1)
    gate, up = Gather(gate_piece, zx_turned, group), Gather(up_piece, zx, group)
    cot_first_other = swap(cot_first, SIDE)
    down_x = Gather(down_piece, near + outer, (), down_rank)
    cot_first_other, cot_last = advance([mix_a, mix_b, down_x], cot_first_other, cot_last)
    tie_chains([gate, up, mix_a, mix_b])

    finish(down_x)
    down_piece = down_x.value()
    while mix_a.left or mix_b.left:
        down_piece, cot_last = advance([mix_a, mix_b, gate, up], down_piece, cot_last)

    inputs = tokens.reshape(row_total, feature_width).astype(jnp.float32)
    cot_full = cot_low.astype(jnp.float32)
    cot_last_other = swap(cot_last, SIDE)
    core_a, core_b = Gather(mix_a.value(), [CORE], mix_a.held), Gather(mix_b.value(), [CORE], mix_b.held)
    step(core_a)
    step(core_b)
    weight_bv = core_a.value().reshape(feature_width, half_width)
    weight_c_out = core_b.value().reshape(feature_width, half_width + 128)
    weight_c = weight_c_out[:, :feature_width]
    weight_out = weight_c_out[:, feature_width:half_width]
    small_whole = weight_c_out[:, half_width : half_width + 2 + tap_count].T.astype(jnp.float32)
    gain_one, gain_two, tap_values = small_whole[0], small_whole[1], small_whole[2:]
    normed_a, scale_a, hidden = normalize(inputs, gain_one)
    hidden_low = hidden.astype(jnp.bfloat16)
    bv_part = dot_plain(hidden_low, weight_bv)
    b_part = bv_part[:, :feature_width]
    v_part = bv_part[:, feature_width:]
    mixed = (b_part * v_part).astype(jnp.bfloat16).reshape(seq_count, local_rows, feature_width)
    mixed, hidden_low, weight_c, down_piece, cot_last_other, *up.arrays = advance(
        [], mixed, hidden_low, weight_c, down_piece, cot_last_other, *up.arrays, first=[gate]
    )
    edge_rows = shifted(mixed[:, local_rows - (tap_count - 1) :, :], "seq", 1)
    c_part = dot_plain(hidden_low, weight_c)
    extended = jnp.concatenate([edge_rows, mixed], axis=1).astype(jnp.float32)
    convolved = tap_values[0] * extended[:, 0:local_rows]
    for offset in range(1, tap_count):
        convolved = convolved + tap_values[offset] * extended[:, offset : offset + local_rows]
    convolved = convolved.reshape(row_total, feature_width)
    gated = (c_part * convolved).astype(jnp.bfloat16)
    after_mix = inputs + dot_plain(gated, weight_out)
    normed_b, scale_b, hidden_b = normalize(after_mix, gain_two)
    hidden_b_low = hidden_b.astype(jnp.bfloat16)
    down_a = Gather(down_piece[..., :down_half], far, near + outer, down_rank)
    down_b = Gather(down_piece[..., down_half:], far[::-1], near + outer, down_rank)
    (hidden_b_low,) = advance([down_a, down_b], hidden_b_low, first=[up], second=[gate])
    finish(gate)
    weight_gate = gate.value().reshape(feature_width, quarter)

    def both_cores(value):
        return jnp.concatenate([value, swap(value, CORE)], axis=0)

    def forward(hidden_rows):
        gate_value = dot_plain(hidden_rows, weight_gate)
        up_value = dot_plain(hidden_rows, weight_up)
        sigmoid_gate = jax.nn.sigmoid(gate_value)
        silu_gate = gate_value * sigmoid_gate
        slope = up_value * (sigmoid_gate * (1.0 + gate_value * (1.0 - sigmoid_gate)))
        active = (silu_gate * up_value).astype(jnp.bfloat16)
        return active, silu_gate.astype(jnp.bfloat16), slope.astype(jnp.bfloat16)

    half_rows = row_total // 2
    hidden_side = [swap(hidden_b_low[:half_rows], SIDE)]
    hidden_near = both_cores(hidden_b_low)
    cot_near = both_cores(cot_low)
    cot_far = both_cores(jnp.concatenate([cot_first_other, cot_last_other], axis=0))
    hidden_near, cot_near, cot_far, hidden_b_low, *hidden_side = advance(
        [], hidden_near, cot_near, cot_far, hidden_b_low, *hidden_side,
        first=[down_a, down_b], second=[up],
    )
    finish(up)
    weight_up = up.value().reshape(feature_width, quarter)
    hidden_side.append(swap(hidden_b_low[half_rows:], SIDE))
    active_near, silu_near, slope_near = forward(hidden_near)
    grad_down_near = dot_first(active_near, cot_near)
    active_near, silu_near, slope_near, grad_down_near, *hidden_side = advance(
        [], active_near, silu_near, slope_near, grad_down_near, *hidden_side,
        second=[down_a, down_b],
    )
    finish(down_a, down_b)
    weight_down = jnp.concatenate(
        [down_a.value().reshape(quarter, down_half), down_b.value().reshape(quarter, down_half)], axis=1
    )

    hidden_far = both_cores(jnp.concatenate(hidden_side, axis=0))
    active_far, silu_far, slope_far = forward(hidden_far)

    def split(gradient, rows):
        return gradient.astype(jnp.bfloat16).reshape((2,) * len(zx) + rows)

    grad_down = split(grad_down_near + dot_first(active_far, cot_far), (-1, feature_width))
    grad_down, hidden_far, active_far, silu_far, slope_far = tie(
        grad_down, hidden_far, active_far, silu_far, slope_far
    )
    grad_down_a = Scatter(grad_down[..., :down_half], x_first + far[1:], zx, down_rank)
    grad_down_b = Scatter(grad_down[..., down_half:], z_first + far[1:], zx, down_rank)

    def backward(cot_rows, silu_gate, slope):
        d_active = dot_second(cot_rows, weight_down)
        d_up = (d_active * silu_gate.astype(jnp.float32)).astype(jnp.bfloat16)
        d_gate = (d_active * slope.astype(jnp.float32)).astype(jnp.bfloat16)
        return d_gate, d_up

    def terms_of(parts):
        def rows(at):
            return sum(dot(left[at], right) for dot, left, right in parts)

        return rows(slice(0, row_total)), rows(slice(row_total, None)).astype(jnp.bfloat16)

    def kept_terms(parts):
        return terms_of(parts)[0]

    def sent_terms(parts):
        return terms_of(parts)[1]

    def one_core(kept, sent):
        return kept + swap(sent, CORE).astype(jnp.float32)

    d_gate_far, d_up_far = backward(cot_far, silu_far, slope_far)
    d_hidden_far = one_core(
        *terms_of([(dot_second, d_gate_far, weight_gate), (dot_second, d_up_far, weight_up)])
    ).astype(jnp.bfloat16)
    out_kept, out_sent = terms_of([(dot_plain, active_far, weight_down)])
    d_hidden_far, d_gate_far, d_up_far, cot_near, out_kept, out_sent, active_near = tie_chains(
        [grad_down_a, grad_down_b],
        d_hidden_far, d_gate_far, d_up_far, cot_near, out_kept, out_sent, active_near,
    )
    d_hidden_side = [swap(d_hidden_far[:half_rows], SIDE)]
    d_gate_near, d_up_near = backward(cot_near, silu_near, slope_near)
    d_hidden_sent = sent_terms(
        [(dot_second, d_gate_near, weight_gate), (dot_second, d_up_near, weight_up)]
    )
    (
        d_hidden_sent, d_hidden_far, d_gate_near, d_gate_far, d_up_near, d_up_far,
        out_kept, out_sent, active_near, *d_hidden_side,
    ) = advance(
        [grad_down_a, grad_down_b],
        d_hidden_sent, d_hidden_far, d_gate_near, d_gate_far, d_up_near, d_up_far,
        out_kept, out_sent, active_near, *d_hidden_side,
    )
    d_hidden_side.append(swap(d_hidden_far[half_rows:], SIDE))
    gate_rows = (2, 2, own_rows, quarter)

    def two_scatters(near_terms, far_terms):
        terms = split(
            dot_first(hidden_near, near_terms) + dot_first(hidden_far, far_terms), gate_rows
        )
        return [
            Scatter(
                lax.index_in_dim(terms, way, len(far) + 1, keepdims=False), dims + far[1:], zx + [SIDE]
            )
            for way, dims in enumerate((x_first, z_first))
        ]

    grad_gate = two_scatters(d_gate_near, d_gate_far)
    d_hidden_kept = kept_terms(
        [(dot_second, d_gate_near, weight_gate), (dot_second, d_up_near, weight_up)]
    )
    out_received = swap(out_sent, CORE)
    (
        d_hidden_kept, d_hidden_sent, out_kept, out_received, d_up_near, d_up_far, active_near,
        *d_hidden_side,
    ) = advance(
        [grad_down_a, grad_down_b],
        d_hidden_kept, d_hidden_sent, out_kept, out_received, d_up_near, d_up_far, active_near,
        *d_hidden_side,
    )
    grad_down = joint([grad_down_a, grad_down_b], -1)
    out_far = (out_kept + out_received.astype(jnp.float32)).astype(jnp.bfloat16)
    out_far, *d_hidden_side = tie_chains([grad_down, *grad_gate], out_far, *d_hidden_side)
    d_hidden_side = jnp.concatenate(d_hidden_side, axis=0)

    out_side = swap(out_far, SIDE)
    d_hidden_b = one_core(d_hidden_kept, d_hidden_sent) + d_hidden_side.astype(jnp.float32)
    d_norm_input, grad_gain_two = norm_back(d_hidden_b, normed_b, scale_b, gain_two)
    d_after = cot_full + d_norm_input
    d_branch = d_after.astype(jnp.bfloat16)
    d_gated = dot_second(d_branch, weight_out)
    d_c = (d_gated * convolved).astype(jnp.bfloat16)
    d_conv = (d_gated * c_part).reshape(seq_count, local_rows, feature_width)
    padded_grad = jnp.pad(d_conv, ((0, 0), (tap_count - 1, tap_count - 1), (0, 0)))
    span = local_rows + tap_count - 1
    d_extended = tap_values[0] * padded_grad[:, tap_count - 1 : tap_count - 1 + span]
    for offset in range(1, tap_count):
        start_at = tap_count - 1 - offset
        d_extended = d_extended + tap_values[offset] * padded_grad[:, start_at : start_at + span]
    edge_terms = d_extended[:, : tap_count - 1, :]
    grad_up = two_scatters(d_up_near, d_up_far)
    held_all = route_a + [CORE]
    shape_all = (2,) * len(held_all) + (own_rows, half_width)
    shape_one = (2,) * len(held_all) + (own_rows, feature_width)
    (
        edge_terms, out_side, d_branch, d_c, d_conv, active_near,
    ) = advance(
        [*grad_gate, grad_down],
        edge_terms, out_side, d_branch, d_c, d_conv, active_near,
    )
    finish(grad_down)
    down_owned, *_ = tie_chains([*grad_gate, *grad_up], grad_down.value().astype(jnp.bfloat16))

    incoming = shifted(edge_terms, "seq", -1)
    grad_out = Scatter(
        dot_first(gated, d_branch).astype(jnp.bfloat16).reshape(shape_one), [CORE] + route_b[::-1], held_all
    )
    grad_c = Scatter(
        dot_first(hidden_low, d_c).astype(jnp.bfloat16).reshape(shape_one), [CORE] + route_b[::-1], held_all
    )
    grad_b = Joint([grad_out, grad_c], -1)
    incoming_full = jnp.pad(incoming, ((0, 0), (local_rows - (tap_count - 1), 0), (0, 0)))
    d_mixed = (d_extended[:, tap_count - 1 :, :] + incoming_full).reshape(row_total, feature_width)
    d_bv = jnp.concatenate(
        [(d_mixed * v_part).astype(jnp.bfloat16), (d_mixed * b_part).astype(jnp.bfloat16)], axis=1
    )
    grad_a = Scatter(
        dot_first(hidden_low, d_bv).astype(jnp.bfloat16).reshape(shape_all),
        [CORE] + route_a[::-1],
        held_all,
    )
    d_bv, d_c, d_conv, out_side, down_owned, active_near = advance(
        [*grad_up, *grad_gate], d_bv, d_c, d_conv, out_side, down_owned, active_near
    )

    grad_gate = joint(grad_gate, 0)
    grad_gate.prepare()
    d_hidden = dot_second(d_bv, weight_bv) + dot_second(d_c, weight_c)
    grad_taps = jnp.stack(
        [
            jnp.sum(d_conv * extended[:, offset : offset + local_rows], axis=(0, 1))
            for offset in range(tap_count)
        ],
        axis=0,
    )
    d_first_norm, grad_gain_one = norm_back(d_hidden, normed_a, scale_a, gain_one)
    grad_tokens = (d_after + d_first_norm).reshape(seq_count, local_rows, feature_width)
    small_terms = jnp.concatenate(
        [grad_gain_one[None, :], grad_gain_two[None, :], grad_taps], axis=0
    )

    small_terms, down_owned, active_near, *grad_gate.ready = advance(
        [grad_a, grad_b, *grad_up],
        small_terms, down_owned, active_near, *grad_gate.ready,
    )
    grad_up = joint(grad_up, 0)
    down_owned, active_near = tie_chains(
        [grad_b, grad_a, grad_gate, grad_up], down_owned, active_near
    )

    for dim in [CORE] + far:
        small_terms = small_terms + swap(small_terms, dim)
    down_owned = quarter_owner_swap(down_owned)
    grad_up.prepare()
    out_kept, out_sent = terms_of([(dot_plain, active_near, weight_down)])
    small_terms, grad_tokens, out_kept, out_sent, down_owned, *grad_up.ready = advance(
        [grad_a, grad_b, grad_gate],
        small_terms, grad_tokens, out_kept, out_sent, down_owned, *grad_up.ready,
    )
    finish(grad_gate)
    tie_chains([grad_up, grad_a, grad_b])

    def owned_rows(joint_chain):
        return jnp.stack([chain.value() for chain in joint_chain.chains])

    def owned_quarters(cores):
        both = jnp.stack(ordered(core, *cores), axis=1)
        mine = lax.dynamic_index_in_dim(both, side, 0, keepdims=False)
        send = lax.dynamic_index_in_dim(both, 1 - side, 0, keepdims=False)
        other = swap(send.astype(jnp.bfloat16), SIDE).astype(jnp.float32)
        low, high = ordered(side, mine, other)
        return jnp.concatenate([low[0], high[0], low[1], high[1]], axis=-1)

    out_own = one_core(out_kept, out_sent)
    gate_core = regroup(owned_rows(grad_gate), 0, core, CORE)
    small_terms, out_own, *gate_core = advance(
        [grad_a, grad_b, grad_up], small_terms, out_own, *gate_core
    )
    finish(grad_up)
    results = after_mix + (out_own + out_side.astype(jnp.float32))
    block_out = results.astype(jnp.bfloat16).reshape(seq_count, local_rows, feature_width)
    gate_owned = owned_quarters(gate_core)
    up_core = regroup(owned_rows(grad_up), 0, core, CORE)
    for dim in near + [SIDE] + outer:
        small_terms = small_terms + swap(small_terms, dim)
    small_terms, gate_owned, block_out, *up_core = advance(
        [grad_a, grad_b], small_terms, gate_owned, block_out, *up_core
    )
    up_owned = owned_quarters(up_core)
    finish(grad_a, grad_b)
    owned_a, owned_b = grad_a.value(), grad_b.value()
    place = lax.axis_index("fsdp") * lax.axis_size("seq") + lax.axis_index("seq")
    small_owned = lax.dynamic_slice_in_dim(small_terms, place * own_rows, own_rows, axis=1)
    return (
        block_out,
        grad_tokens,
        small_owned[0],
        jnp.concatenate(
            [owned_a[:, :feature_width], owned_b[:, feature_width:], owned_a[:, feature_width:]],
            axis=1,
        ),
        small_owned[2:],
        owned_b[:, :feature_width],
        small_owned[1],
        gate_owned,
        up_owned,
        down_owned.astype(jnp.float32),
    )


def solution(mesh):
    return jax.shard_map(
        body,
        mesh=mesh,
        in_specs=(
            P("fsdp", "seq", None),
            P(("fsdp", "seq")),
            P(("fsdp", "seq"), None),
            P(None, ("fsdp", "seq")),
            P(("fsdp", "seq"), None),
            P(("fsdp", "seq")),
            P(("fsdp", "seq"), None),
            P(("fsdp", "seq"), None),
            P(("fsdp", "seq"), None),
            P("fsdp", "seq", None),
        ),
        out_specs=(
            P("fsdp", "seq", None),
            P("fsdp", "seq", None),
            P(("fsdp", "seq")),
            P(("fsdp", "seq"), None),
            P(None, ("fsdp", "seq")),
            P(("fsdp", "seq"), None),
            P(("fsdp", "seq")),
            P(("fsdp", "seq"), None),
            P(("fsdp", "seq"), None),
            P(("fsdp", "seq"), None),
        ),
        check_vma=False,
    )
```

```python
import jax
import jax.numpy as jnp
from jax import lax
from jax.sharding import PartitionSpec as P

EPSILON = 1e-05
CORE = ("fsdp", 0)
SIDE = ("seq", 0)
WAY = ("way", 0)


def shifted(shard, axis, by):
    size = lax.axis_size(axis)
    pairs = [(i, i + by) for i in range(size) if 0 <= i + by < size]
    return lax.ppermute(shard, axis, pairs)


def bit_count(axis):
    return lax.axis_size(axis).bit_length() - 1


def my_bit(dim):
    axis, bit = dim
    return (lax.axis_index(axis) >> bit) & 1


def swap(value, dim):
    axis, bit = dim
    return lax.ppermute(value, axis, [(i, i ^ (1 << bit)) for i in range(lax.axis_size(axis))])


def rank(dim):
    axis, bit = dim
    return (0 if axis == "fsdp" else 1, -bit)


def down_rank(dim):
    top = bit_count("fsdp") - 1
    return rank({("fsdp", top): CORE, ("fsdp", top - 1): SIDE}.get(dim, dim))


def tie(*values):
    return lax.optimization_barrier(values)


class Chain:
    def __init__(self, dims, held, order):
        self.left, self.held, self.order = list(dims), list(held), order
        self.parts, self.ready = [], []

    def prepare(self):
        self.ready = [self.sent()]

    def start(self):
        if self.left:
            sent = self.ready.pop() if self.ready else self.sent()
            self.parts = [swap(sent, self.left[0])]

    def start_half(self, half):
        if self.left:
            sent = self.sent()
            middle = sent.shape[0] // 2
            part = swap(sent[middle:] if half else sent[:middle], self.left[0])
            self.parts = self.parts + [part] if half else [part]

    def merge(self):
        if self.left:
            other = self.parts[0] if len(self.parts) == 1 else jnp.concatenate(self.parts, axis=0)
            self.parts = []
            self.take(self.left.pop(0), other)


class Gather(Chain):
    def __init__(self, piece, dims, held=(), order=rank):
        super().__init__(dims, held, order)
        self.arrays = [piece]

    def value(self):
        return self.arrays[0]

    def sent(self):
        return self.arrays[0]

    def take(self, dim, other):
        axis = sum(self.order(h) < self.order(dim) for h in self.held)
        high, mine = my_bit(dim) == 1, self.arrays[0]
        self.arrays = [
            jnp.stack([jnp.where(high, other, mine), jnp.where(high, mine, other)], axis=axis)
        ]
        self.held.append(dim)


class Scatter(Chain):
    def __init__(self, terms, dims, held, order=rank):
        super().__init__(dims, sorted(held, key=order), order)
        self.arrays, self.cuts = [terms], [[]]

    def summed(self, further):
        total = 0.0
        for array, cuts in zip(self.arrays, self.cuts):
            for axis, index in cuts + further:
                array = lax.dynamic_index_in_dim(array, index, axis, keepdims=False)
            total = total + array.astype(jnp.float32)
        return total

    def value(self):
        return self.summed([])

    def sent(self):
        dim = self.left[0]
        return self.summed([(self.held.index(dim), 1 - my_bit(dim))]).astype(jnp.bfloat16)

    def take(self, dim, other):
        cut = (self.held.index(dim), my_bit(dim))
        self.cuts = [cuts + [cut] for cuts in self.cuts] + [[]]
        self.arrays = self.arrays + [other]
        self.held.remove(dim)


class Joint(Chain):
    def __init__(self, chains, axis):
        super().__init__(chains[0].left, chains[0].held, chains[0].order)
        self.chains, self.axis = chains, axis

    @property
    def arrays(self):
        return [array for chain in self.chains for array in chain.arrays]

    @arrays.setter
    def arrays(self, values):
        for chain in self.chains:
            chain.arrays, values = values[: len(chain.arrays)], values[len(chain.arrays) :]

    def sent(self):
        return jnp.concatenate([chain.sent() for chain in self.chains], axis=self.axis)

    def take(self, dim, other):
        for chain, part in zip(self.chains, jnp.split(other, len(self.chains), axis=self.axis)):
            chain.left.pop(0)
            chain.take(dim, part)

    def value(self):
        return jnp.concatenate([chain.value() for chain in self.chains], axis=self.axis)


def tie_chains(chains, *others, parts=True):
    flat = [array for chain in chains for array in chain.arrays]
    flat += [array for chain in chains for array in chain.ready]
    if parts:
        flat += [part for chain in chains for part in chain.parts]
    tied = list(tie(*flat, *others))
    for chain in chains:
        chain.arrays = [tied.pop(0) for _ in chain.arrays]
    for chain in chains:
        chain.ready = [tied.pop(0) for _ in chain.ready]
    for chain in chains if parts else ():
        chain.parts = [tied.pop(0) for _ in chain.parts]
    return tied


def advance(chains, *others, first=(), second=()):
    for chain in chains:
        chain.start()
    for chain in first:
        chain.start_half(0)
    for chain in second:
        chain.start_half(1)
    every = [*chains, *first, *second]
    others = tie_chains(every, *others, parts=False)
    for chain in [*chains, *second]:
        chain.merge()
    return tie_chains(every, *others)


def step(chain):
    chain.start()
    chain.merge()


def joint(chains, axis):
    for chain in chains:
        while chain.left[:1] != chains[0].left[-1:]:
            step(chain)
    return Joint(chains, axis)


def finish(*chains):
    for chain in chains:
        while chain.left:
            step(chain)


def normalize(values, gain):
    scale = lax.rsqrt(jnp.mean(values * values, axis=-1, keepdims=True) + EPSILON)
    normalized_rows = values * scale
    return (normalized_rows, scale, normalized_rows * gain)


def norm_back(d_hidden, normalized_rows, scale, gain):
    norm_gradient = d_hidden * gain
    grad_gain = jnp.sum(d_hidden * normalized_rows, axis=0)
    d_input = scale * (
        norm_gradient
        - normalized_rows * jnp.mean(norm_gradient * normalized_rows, axis=-1, keepdims=True)
    )
    return (d_input, grad_gain)


def dot_plain(left_segment, right_segment):
    return jnp.dot(left_segment, right_segment, preferred_element_type=jnp.float32)


def dot_first(left_segment, right_segment):
    return lax.dot_general(
        left_segment, right_segment, (((0,), (0,)), ((), ())), preferred_element_type=jnp.float32
    )


def dot_second(left_segment, right_segment):
    return lax.dot_general(
        left_segment, right_segment, (((1,), (1,)), ((), ())), preferred_element_type=jnp.float32
    )


def quarter_owner_swap(value):
    fsdp, seq = lax.axis_size("fsdp"), lax.axis_size("seq")
    top = bit_count("fsdp") - 1
    pairs = []
    for device in range(fsdp * seq):
        f, s = divmod(device, seq)
        high, low = (f >> top) & 1, (f >> (top - 1)) & 1
        core, side = f & 1, s & 1
        f2 = (f & ~((1 << top) | (1 << (top - 1)) | 1)) | (core << top) | (side << (top - 1)) | high
        pairs.append((device, f2 * seq + ((s & ~1) | low)))
    return lax.ppermute(value, ("fsdp", "seq"), pairs)


def body(tokens, gain_a, mix_in, conv_tap, mix_out, gain_b, ff_gate, ff_up, ff_down, cotangent):
    seq_count, local_rows, feature_width = tokens.shape
    row_total = seq_count * local_rows
    tap_count = conv_tap.shape[0]
    own_rows = mix_in.shape[0]
    hidden_units = ff_gate.shape[1]
    quarter = hidden_units // 4
    core, side = my_bit(CORE), my_bit(SIDE)
    near = [("fsdp", 1)]
    far = [("fsdp", b) for b in range(2, bit_count("fsdp"))]
    outer = [("seq", b) for b in range(1, bit_count("seq"))]
    zx, zx_turned = far + near + outer, far[::-1] + near + outer
    x_first, z_first = outer + near + far[:1], far[:1] + outer + near
    route_a, route_b = far + near + outer + [SIDE], far[::-1] + [SIDE] + outer + near
    group = [CORE, SIDE]
    half_width = 2 * feature_width
    down_half = feature_width // 2

    def ordered(pair_bit, mine, other):
        high = pair_bit == 1
        return jnp.where(high, other, mine), jnp.where(high, mine, other)

    small = jnp.concatenate([gain_a[None], gain_b[None], conv_tap], axis=0).T
    small = jnp.pad(small, ((0, 0), (0, 128 - small.shape[1])))
    mix_a = Gather(
        jnp.concatenate([mix_in[:, :feature_width], mix_in[:, 2 * feature_width :]], axis=1), route_a
    )
    mix_b = Gather(
        jnp.concatenate([mix_in[:, feature_width : 2 * feature_width], mix_out, small], axis=1),
        route_b,
    )

    def quarters(shard):
        return jnp.stack([shard[:, q * quarter : (q + 1) * quarter] for q in range(4)]).reshape(
            2, 2, own_rows, quarter
        )

    def regroup(parts, axis, bit, dim):
        mine = lax.dynamic_index_in_dim(parts, bit, axis, keepdims=False)
        other = swap(lax.dynamic_index_in_dim(parts, 1 - bit, axis, keepdims=False), dim)
        return mine, other

    gate_up = regroup(jnp.stack([quarters(ff_gate), quarters(ff_up)]), 2, side, SIDE)
    cot_low = cotangent.reshape(row_total, feature_width)
    cot_first, cot_last = cot_low[: row_total // 2], cot_low[row_total // 2 :]
    down_piece = quarter_owner_swap(ff_down)
    *gate_up, cot_first, down_piece = advance([mix_a, mix_b], *gate_up, cot_first, down_piece)

    gate_up = regroup(jnp.stack(ordered(side, *gate_up), axis=2), 1, core, CORE)
    gate_piece, up_piece = jnp.stack(ordered(core, *gate_up), axis=1)
    gate, up = Gather(gate_piece, zx_turned, group), Gather(up_piece, zx, group)
    cot_first_other = swap(cot_first, SIDE)
    down_x = Gather(down_piece, near + outer, (), down_rank)
    cot_first_other, cot_last = advance([mix_a, mix_b, down_x], cot_first_other, cot_last)
    tie_chains([gate, up, mix_a, mix_b])

    finish(down_x)
    down_piece = down_x.value()
    while mix_a.left or mix_b.left:
        down_piece, cot_last = advance([mix_a, mix_b, gate, up], down_piece, cot_last)

    inputs = tokens.reshape(row_total, feature_width).astype(jnp.float32)
    cot_full = cot_low.astype(jnp.float32)
    cot_last_other = swap(cot_last, SIDE)
    core_a, core_b = Gather(mix_a.value(), [CORE], mix_a.held), Gather(mix_b.value(), [CORE], mix_b.held)
    step(core_a)
    step(core_b)
    weight_bv = core_a.value().reshape(feature_width, half_width)
    weight_c_out = core_b.value().reshape(feature_width, half_width + 128)
    weight_c = weight_c_out[:, :feature_width]
    weight_out = weight_c_out[:, feature_width:half_width]
    small_whole = weight_c_out[:, half_width : half_width + 2 + tap_count].T.astype(jnp.float32)
    gain_one, gain_two, tap_values = small_whole[0], small_whole[1], small_whole[2:]
    normed_a, scale_a, hidden = normalize(inputs, gain_one)
    hidden_low = hidden.astype(jnp.bfloat16)
    bv_part = dot_plain(hidden_low, weight_bv)
    b_part = bv_part[:, :feature_width]
    v_part = bv_part[:, feature_width:]
    mixed = (b_part * v_part).astype(jnp.bfloat16).reshape(seq_count, local_rows, feature_width)
    mixed, hidden_low, weight_c, down_piece, cot_last_other, *up.arrays = advance(
        [], mixed, hidden_low, weight_c, down_piece, cot_last_other, *up.arrays, first=[gate]
    )
    edge_rows = shifted(mixed[:, local_rows - (tap_count - 1) :, :], "seq", 1)
    c_part = dot_plain(hidden_low, weight_c)
    extended = jnp.concatenate([edge_rows, mixed], axis=1).astype(jnp.float32)
    convolved = tap_values[0] * extended[:, 0:local_rows]
    for offset in range(1, tap_count):
        convolved = convolved + tap_values[offset] * extended[:, offset : offset + local_rows]
    convolved = convolved.reshape(row_total, feature_width)
    gated = (c_part * convolved).astype(jnp.bfloat16)
    after_mix = inputs + dot_plain(gated, weight_out)
    normed_b, scale_b, hidden_b = normalize(after_mix, gain_two)
    hidden_b_low = hidden_b.astype(jnp.bfloat16)
    down_a = Gather(down_piece[..., :down_half], far, near + outer, down_rank)
    down_b = Gather(down_piece[..., down_half:], far[::-1], near + outer, down_rank)
    (hidden_b_low,) = advance([down_a, down_b], hidden_b_low, first=[up], second=[gate])
    finish(gate)
    weight_gate = gate.value().reshape(feature_width, quarter)

    def both_cores(value):
        return jnp.concatenate([value, swap(value, CORE)], axis=0)

    def forward(hidden_rows):
        gate_value = dot_plain(hidden_rows, weight_gate)
        up_value = dot_plain(hidden_rows, weight_up)
        sigmoid_gate = jax.nn.sigmoid(gate_value)
        silu_gate = gate_value * sigmoid_gate
        slope = up_value * (sigmoid_gate * (1.0 + gate_value * (1.0 - sigmoid_gate)))
        active = (silu_gate * up_value).astype(jnp.bfloat16)
        return active, silu_gate.astype(jnp.bfloat16), slope.astype(jnp.bfloat16)

    half_rows = row_total // 2
    hidden_side = [swap(hidden_b_low[:half_rows], SIDE)]
    hidden_near = both_cores(hidden_b_low)
    cot_near = both_cores(cot_low)
    cot_far = both_cores(jnp.concatenate([cot_first_other, cot_last_other], axis=0))
    hidden_near, cot_near, cot_far, hidden_b_low, *hidden_side = advance(
        [], hidden_near, cot_near, cot_far, hidden_b_low, *hidden_side,
        first=[down_a, down_b], second=[up],
    )
    finish(up)
    weight_up = up.value().reshape(feature_width, quarter)
    hidden_side.append(swap(hidden_b_low[half_rows:], SIDE))
    active_near, silu_near, slope_near = forward(hidden_near)
    grad_down_near = dot_first(active_near, cot_near)
    active_near, silu_near, slope_near, grad_down_near, *hidden_side = advance(
        [], active_near, silu_near, slope_near, grad_down_near, *hidden_side,
        second=[down_a, down_b],
    )
    finish(down_a, down_b)
    weight_down = jnp.concatenate(
        [down_a.value().reshape(quarter, down_half), down_b.value().reshape(quarter, down_half)], axis=1
    )

    hidden_far = both_cores(jnp.concatenate(hidden_side, axis=0))
    active_far, silu_far, slope_far = forward(hidden_far)

    def split(gradient, rows):
        return gradient.astype(jnp.bfloat16).reshape((2,) * len(zx) + rows)

    grad_down = split(grad_down_near + dot_first(active_far, cot_far), (-1, feature_width))
    grad_down, hidden_far, active_far, silu_far, slope_far = tie(
        grad_down, hidden_far, active_far, silu_far, slope_far
    )
    grad_down_a = Scatter(grad_down[..., :down_half], x_first + far[1:], zx, down_rank)
    grad_down_b = Scatter(grad_down[..., down_half:], z_first + far[1:], zx, down_rank)

    def backward(cot_rows, silu_gate, slope):
        d_active = dot_second(cot_rows, weight_down)
        d_up = (d_active * silu_gate.astype(jnp.float32)).astype(jnp.bfloat16)
        d_gate = (d_active * slope.astype(jnp.float32)).astype(jnp.bfloat16)
        return d_gate, d_up

    def terms_of(parts):
        def rows(at):
            return sum(dot(left[at], right) for dot, left, right in parts)

        return rows(slice(0, row_total)), rows(slice(row_total, None)).astype(jnp.bfloat16)

    def kept_terms(parts):
        return terms_of(parts)[0]

    def sent_terms(parts):
        return terms_of(parts)[1]

    def one_core(kept, sent):
        return kept + swap(sent, CORE).astype(jnp.float32)

    d_gate_far, d_up_far = backward(cot_far, silu_far, slope_far)
    d_hidden_far = one_core(
        *terms_of([(dot_second, d_gate_far, weight_gate), (dot_second, d_up_far, weight_up)])
    ).astype(jnp.bfloat16)
    out_kept, out_sent = terms_of([(dot_plain, active_far, weight_down)])
    d_hidden_far, d_gate_far, d_up_far, cot_near, out_kept, out_sent, active_near = tie_chains(
        [grad_down_a, grad_down_b],
        d_hidden_far, d_gate_far, d_up_far, cot_near, out_kept, out_sent, active_near,
    )
    d_hidden_side = [swap(d_hidden_far[:half_rows], SIDE)]
    d_gate_near, d_up_near = backward(cot_near, silu_near, slope_near)
    d_hidden_sent = sent_terms(
        [(dot_second, d_gate_near, weight_gate), (dot_second, d_up_near, weight_up)]
    )
    (
        d_hidden_sent, d_hidden_far, d_gate_near, d_gate_far, d_up_near, d_up_far,
        out_kept, out_sent, active_near, *d_hidden_side,
    ) = advance(
        [grad_down_a, grad_down_b],
        d_hidden_sent, d_hidden_far, d_gate_near, d_gate_far, d_up_near, d_up_far,
        out_kept, out_sent, active_near, *d_hidden_side,
    )
    d_hidden_side.append(swap(d_hidden_far[half_rows:], SIDE))
    gate_rows = (2, 2, own_rows, quarter)

    def two_scatters(near_terms, far_terms):
        terms = split(
            dot_first(hidden_near, near_terms) + dot_first(hidden_far, far_terms), gate_rows
        )
        return [
            Scatter(
                lax.index_in_dim(terms, way, len(far) + 1, keepdims=False), dims + far[1:], zx + [SIDE]
            )
            for way, dims in enumerate((x_first, z_first))
        ]

    grad_gate = two_scatters(d_gate_near, d_gate_far)
    d_hidden_kept = kept_terms(
        [(dot_second, d_gate_near, weight_gate), (dot_second, d_up_near, weight_up)]
    )
    out_received = swap(out_sent, CORE)
    (
        d_hidden_kept, d_hidden_sent, out_kept, out_received, d_up_near, d_up_far, active_near,
        *d_hidden_side,
    ) = advance(
        [grad_down_a, grad_down_b],
        d_hidden_kept, d_hidden_sent, out_kept, out_received, d_up_near, d_up_far, active_near,
        *d_hidden_side,
    )
    grad_down = joint([grad_down_a, grad_down_b], -1)
    out_far = (out_kept + out_received.astype(jnp.float32)).astype(jnp.bfloat16)
    out_far, *d_hidden_side = tie_chains([grad_down, *grad_gate], out_far, *d_hidden_side)
    d_hidden_side = jnp.concatenate(d_hidden_side, axis=0)

    out_side = swap(out_far, SIDE)
    d_hidden_b = one_core(d_hidden_kept, d_hidden_sent) + d_hidden_side.astype(jnp.float32)
    d_norm_input, grad_gain_two = norm_back(d_hidden_b, normed_b, scale_b, gain_two)
    d_after = cot_full + d_norm_input
    d_branch = d_after.astype(jnp.bfloat16)
    d_gated = dot_second(d_branch, weight_out)
    d_c = (d_gated * convolved).astype(jnp.bfloat16)
    d_conv = (d_gated * c_part).reshape(seq_count, local_rows, feature_width)
    padded_grad = jnp.pad(d_conv, ((0, 0), (tap_count - 1, tap_count - 1), (0, 0)))
    span = local_rows + tap_count - 1
    d_extended = tap_values[0] * padded_grad[:, tap_count - 1 : tap_count - 1 + span]
    for offset in range(1, tap_count):
        start_at = tap_count - 1 - offset
        d_extended = d_extended + tap_values[offset] * padded_grad[:, start_at : start_at + span]
    edge_terms = d_extended[:, : tap_count - 1, :]
    grad_up = two_scatters(d_up_near, d_up_far)
    held_all = route_a + [CORE]
    shape_all = (2,) * len(held_all) + (own_rows, half_width)
    shape_one = (2,) * len(held_all) + (own_rows, feature_width)
    (
        edge_terms, out_side, d_branch, d_c, d_conv, active_near,
    ) = advance(
        [*grad_gate, grad_down],
        edge_terms, out_side, d_branch, d_c, d_conv, active_near,
    )
    finish(grad_down)
    down_owned, *_ = tie_chains([*grad_gate, *grad_up], grad_down.value().astype(jnp.bfloat16))

    incoming = shifted(edge_terms, "seq", -1)
    grad_out = Scatter(
        dot_first(gated, d_branch).astype(jnp.bfloat16).reshape(shape_one), [CORE] + route_b[::-1], held_all
    )
    grad_c = Scatter(
        dot_first(hidden_low, d_c).astype(jnp.bfloat16).reshape(shape_one), [CORE] + route_b[::-1], held_all
    )
    grad_b = Joint([grad_out, grad_c], -1)
    incoming_full = jnp.pad(incoming, ((0, 0), (local_rows - (tap_count - 1), 0), (0, 0)))
    d_mixed = (d_extended[:, tap_count - 1 :, :] + incoming_full).reshape(row_total, feature_width)
    d_bv = jnp.concatenate(
        [(d_mixed * v_part).astype(jnp.bfloat16), (d_mixed * b_part).astype(jnp.bfloat16)], axis=1
    )
    grad_a = Scatter(
        dot_first(hidden_low, d_bv).astype(jnp.bfloat16).reshape(shape_all),
        [CORE] + route_a[::-1],
        held_all,
    )
    d_bv, d_c, d_conv, out_side, down_owned, active_near = advance(
        [*grad_up, *grad_gate], d_bv, d_c, d_conv, out_side, down_owned, active_near
    )

    grad_gate = joint(grad_gate, 0)
    grad_gate.prepare()
    d_hidden = dot_second(d_bv, weight_bv) + dot_second(d_c, weight_c)
    grad_taps = jnp.stack(
        [
            jnp.sum(d_conv * extended[:, offset : offset + local_rows], axis=(0, 1))
            for offset in range(tap_count)
        ],
        axis=0,
    )
    d_first_norm, grad_gain_one = norm_back(d_hidden, normed_a, scale_a, gain_one)
    grad_tokens = (d_after + d_first_norm).reshape(seq_count, local_rows, feature_width)
    small_terms = jnp.concatenate(
        [grad_gain_one[None, :], grad_gain_two[None, :], grad_taps], axis=0
    )

    down_owned = quarter_owner_swap(down_owned)
    small_terms, down_owned, active_near, *grad_gate.ready = advance(
        [grad_a, grad_b, *grad_up],
        small_terms, down_owned, active_near, *grad_gate.ready,
    )
    grad_up = joint(grad_up, 0)
    down_owned, active_near = tie_chains(
        [grad_b, grad_a, grad_gate, grad_up], down_owned, active_near
    )

    for dim in [CORE] + far:
        small_terms = small_terms + swap(small_terms, dim)
    grad_up.prepare()
    out_kept, out_sent = terms_of([(dot_plain, active_near, weight_down)])
    small_terms, grad_tokens, out_kept, out_sent, down_owned, *grad_up.ready = advance(
        [grad_a, grad_b, grad_gate],
        small_terms, grad_tokens, out_kept, out_sent, down_owned, *grad_up.ready,
    )
    finish(grad_gate)
    tie_chains([grad_up, grad_a, grad_b])

    def owned_rows(joint_chain):
        return jnp.stack([chain.value() for chain in joint_chain.chains])

    def owned_quarters(cores):
        both = jnp.stack(ordered(core, *cores), axis=1)
        mine = lax.dynamic_index_in_dim(both, side, 0, keepdims=False)
        send = lax.dynamic_index_in_dim(both, 1 - side, 0, keepdims=False)
        other = swap(send.astype(jnp.bfloat16), SIDE).astype(jnp.float32)
        low, high = ordered(side, mine, other)
        return jnp.concatenate([low[0], high[0], low[1], high[1]], axis=-1)

    out_own = one_core(out_kept, out_sent)
    gate_core = regroup(owned_rows(grad_gate), 0, core, CORE)
    small_terms, out_own, *gate_core = advance(
        [grad_a, grad_b, grad_up], small_terms, out_own, *gate_core
    )
    finish(grad_up)
    results = after_mix + (out_own + out_side.astype(jnp.float32))
    block_out = results.astype(jnp.bfloat16).reshape(seq_count, local_rows, feature_width)
    gate_owned = owned_quarters(gate_core)
    up_core = regroup(owned_rows(grad_up), 0, core, CORE)
    for dim in near + [SIDE] + outer:
        small_terms = small_terms + swap(small_terms, dim)
    small_terms, gate_owned, block_out, *up_core = advance(
        [grad_a, grad_b], small_terms, gate_owned, block_out, *up_core
    )
    up_owned = owned_quarters(up_core)
    finish(grad_a, grad_b)
    owned_a, owned_b = grad_a.value(), grad_b.value()
    place = lax.axis_index("fsdp") * lax.axis_size("seq") + lax.axis_index("seq")
    small_owned = lax.dynamic_slice_in_dim(small_terms, place * own_rows, own_rows, axis=1)
    return (
        block_out,
        grad_tokens,
        small_owned[0],
        jnp.concatenate(
            [owned_a[:, :feature_width], owned_b[:, feature_width:], owned_a[:, feature_width:]],
            axis=1,
        ),
        small_owned[2:],
        owned_b[:, :feature_width],
        small_owned[1],
        gate_owned,
        up_owned,
        down_owned.astype(jnp.float32),
    )


def solution(mesh):
    return jax.shard_map(
        body,
        mesh=mesh,
        in_specs=(
            P("fsdp", "seq", None),
            P(("fsdp", "seq")),
            P(("fsdp", "seq"), None),
            P(None, ("fsdp", "seq")),
            P(("fsdp", "seq"), None),
            P(("fsdp", "seq")),
            P(("fsdp", "seq"), None),
            P(("fsdp", "seq"), None),
            P(("fsdp", "seq"), None),
            P("fsdp", "seq", None),
        ),
        out_specs=(
            P("fsdp", "seq", None),
            P("fsdp", "seq", None),
            P(("fsdp", "seq")),
            P(("fsdp", "seq"), None),
            P(None, ("fsdp", "seq")),
            P(("fsdp", "seq"), None),
            P(("fsdp", "seq")),
            P(("fsdp", "seq"), None),
            P(("fsdp", "seq"), None),
            P(("fsdp", "seq"), None),
        ),
        check_vma=False,
    )
```
